32 devices in a mesh: gx: 4 (over z), gy: 2 (over y), gz: 4 (over x, core).
Axes of the slice: x: 2, y: 2, z: 4, core: 2. Of those that a mesh axis runs over, the one named last changes fastest.
Arguments:
- snapshot: float32 [512, 320, 512], P('gx', 'gy', 'gz'), may hold values from -40 to 40
Outputs:
- basis: float32 [512, 128], P('gx')
- core: float32 [128, 320, 512], P('gx', 'gy', 'gz')
The draws below stay inside these ranges and needn't reach their ends.
All inputs are finite; a program needn't handle non-finite values.
Results may differ from the reference program's by a relative error of at most 0.0002.
Values sent between devices are 32-bit elements; how exact they have to be, the bound alone decides.
No kernel may reach another device: no remote copies, remote signals or barrier semaphores. Data moves between devices by JAX's collectives and lax.ppermute only.
A program may use at most 64 MiB of HBM per device.

```python
import jax
import jax.numpy as jnp
from jax import lax

NX = 512
RANK = 128
ITERS = 2
NY = 320
NZ = 512


def draw_snapshot(key, part):
    key_left, key_right, key_noise = jax.random.split(key, 3)
    left = jax.random.normal(key_left, (NX, RANK), jnp.float32)
    right = jax.random.normal(key_right, (RANK, NY * NZ), jnp.float32)
    signal = jnp.dot(left, right, precision=lax.Precision.HIGHEST) / jnp.sqrt(jnp.float32(RANK))
    noise = jax.random.normal(key_noise, (NX, NY * NZ), jnp.float32)
    field = 3.0 * signal + noise
    return jnp.clip(field, -40.0, 40.0).reshape(NX, NY, NZ)


def setup_inputs(seed: int = 0) -> dict:
    splits = jax.random.split(jax.random.key(seed), 2)
    return {
        "snapshot": draw_snapshot(jax.random.fold_in(splits[1], 71), 0),
    }


def orthonormal(matrix):
    cross = jnp.dot(matrix.T.astype(jnp.float32), matrix.astype(jnp.float32), precision=lax.Precision.HIGHEST, preferred_element_type=jnp.float32)
    lower = jnp.linalg.cholesky(cross)
    return jax.scipy.linalg.solve_triangular(lower, matrix.T, lower=True).T

def reference(snapshot):
    unfold = snapshot.reshape(NX, NY * NZ)
    gram = jnp.dot(unfold.astype(jnp.float32), unfold.T.astype(jnp.float32), precision=lax.Precision.HIGHEST, preferred_element_type=jnp.float32)
    factor = jnp.linalg.cholesky(gram)
    basis = orthonormal(factor[:, :RANK])
    for step in range(ITERS):
        inner = jnp.dot(factor.T.astype(jnp.float32), basis.astype(jnp.float32), precision=lax.Precision.HIGHEST, preferred_element_type=jnp.float32)
        basis = orthonormal(jnp.dot(factor.astype(jnp.float32), inner.astype(jnp.float32), precision=lax.Precision.HIGHEST, preferred_element_type=jnp.float32))
    core = jnp.dot(basis.T.astype(jnp.float32), unfold.astype(jnp.float32), precision=lax.Precision.HIGHEST, preferred_element_type=jnp.float32)
    return (basis, core.reshape(RANK, NY, NZ))
```

```python
import functools

import jax
import jax.numpy as jnp
from jax import lax
from jax.experimental import pallas as pl
from jax.experimental.pallas import tpu as pltpu
from jax.sharding import PartitionSpec as P

RANK = 128
ITERS = 2
BLOCK = 128
AXES = ("gx", "gy", "gz")


def product(left, right):
    return jnp.dot(left, right, precision=lax.Precision.HIGHEST, preferred_element_type=jnp.float32)


def split(value):
    high = value.astype(jnp.bfloat16)
    low = (value - high.astype(jnp.float32)).astype(jnp.bfloat16)
    return high, low


def dot_t(left, right):
    return lax.dot_general(left, right, (((1,), (1,)), ((), ())), preferred_element_type=jnp.float32)


def dot_n(left, right):
    return lax.dot_general(left, right, (((1,), (0,)), ((), ())), preferred_element_type=jnp.float32)


def gram_kernel(first, groups, steps, xlocal, zlocal, *refs):
    if first:
        rows_ref, out_ref, high_ref, low_ref = refs
        old_ref = None
    else:
        rows_ref, old_ref, out_ref, high_ref, low_ref = refs
    for group in range(groups):
        for step in range(steps):
            high, low = split(rows_ref[group, step])
            at = (slice(group * xlocal, (group + 1) * xlocal), slice(step * zlocal, (step + 1) * zlocal))
            high_ref[at] = high
            low_ref[at] = low
    count = groups * xlocal // BLOCK
    slot = 0
    for row in range(count):
        mine = slice(row * BLOCK, (row + 1) * BLOCK)
        upto = slice(0, (row + 1) * BLOCK)
        total = dot_t(high_ref[mine, :], high_ref[upto, :])
        total += dot_t(high_ref[mine, :], low_ref[upto, :])
        total += dot_t(low_ref[mine, :], high_ref[upto, :])
        for column in range(row + 1):
            block = total[:, column * BLOCK : (column + 1) * BLOCK]
            out_ref[slot] = block if old_ref is None else block + old_ref[slot]
            slot += 1


def gram_step(rows, old):
    groups, steps, xlocal, zlocal = rows.shape
    order = groups * xlocal
    count = order // BLOCK
    slots = count * (count + 1) // 2
    first = old is None
    vmem = pl.BlockSpec(memory_space=pltpu.VMEM)
    half = jax.ShapeDtypeStruct((order, steps * zlocal), jnp.bfloat16)
    operands = (rows,) if first else (rows, old)
    return pl.pallas_call(
        functools.partial(gram_kernel, first, groups, steps, xlocal, zlocal),
        out_shape=(jax.ShapeDtypeStruct((slots, BLOCK, BLOCK), jnp.float32), half, half),
        in_specs=[vmem] * len(operands),
        out_specs=(vmem, vmem, vmem),
        input_output_aliases={} if first else {1: 0},
        compiler_params=pltpu.CompilerParams(vmem_limit_bytes=48 * 2**20),
        cost_estimate=pl.CostEstimate(flops=6 * order * order * steps * zlocal, bytes_accessed=rows.size * 8, transcendentals=0),
    )(*operands)


def core_kernel(steps, zlocal, turned_ref, high_ref, low_ref, out_ref):
    high, low = split(turned_ref[...])
    total = dot_n(high, high_ref[...]) + dot_n(high, low_ref[...]) + dot_n(low, high_ref[...])
    for step in range(steps):
        out_ref[:, step, :] = total[:, step * zlocal : (step + 1) * zlocal]


def core_step(turned, high, low, zlocal):
    steps = high.shape[1] // zlocal
    vmem = pl.BlockSpec(memory_space=pltpu.VMEM)
    return pl.pallas_call(
        functools.partial(core_kernel, steps, zlocal),
        out_shape=jax.ShapeDtypeStruct((turned.shape[0], steps, zlocal), jnp.float32),
        in_specs=[vmem] * 3,
        out_specs=vmem,
        compiler_params=pltpu.CompilerParams(vmem_limit_bytes=48 * 2**20),
        cost_estimate=pl.CostEstimate(flops=6 * turned.size * steps * zlocal, bytes_accessed=high.size * 6, transcendentals=0),
    )(turned, high, low)


def total_sum(blocks):
    devices = lax.axis_size(AXES)
    shape = blocks.shape
    flat = blocks.reshape(-1, BLOCK)
    rows = flat.shape[0]
    share = -(-rows // devices)
    flat = jnp.pad(flat, ((0, share * devices - rows), (0, 0)))
    parts = lax.all_to_all(flat.reshape(devices, share, BLOCK), AXES, split_axis=0, concat_axis=0, tiled=True)
    mine = jnp.sum(parts, axis=0)
    spread = jnp.broadcast_to(mine[None], (devices, share, BLOCK))
    whole = lax.all_to_all(spread, AXES, split_axis=0, concat_axis=0, tiled=True)
    return whole.reshape(-1, BLOCK)[:rows].reshape(shape)


def orthonormal(matrix):
    lower = jnp.linalg.cholesky(product(matrix.T, matrix))
    return jax.scipy.linalg.solve_triangular(lower, matrix.T, lower=True).T


def assemble(blocks, count):
    rows = []
    for row in range(count):
        line = []
        for column in range(count):
            high, low = max(row, column), min(row, column)
            block = blocks[high * (high + 1) // 2 + low]
            line.append(block if row >= column else block.T)
        rows.append(jnp.concatenate(line, axis=1))
    return jnp.concatenate(rows, axis=0)


def chunk_count(per):
    return max(k for k in range(1, 6) if per % k == 0)


def local(snapshot):
    xlocal, ylocal, zlocal = snapshot.shape
    groups = lax.axis_size("gx")
    order = groups * xlocal
    chunks = chunk_count(ylocal // groups)
    wide = ylocal // chunks
    steps = wide // groups
    halves = []
    total = None
    for chunk in range(chunks):
        piece = jnp.transpose(snapshot[:, chunk * wide : (chunk + 1) * wide, :], (1, 0, 2))
        rows = lax.all_to_all(piece, "gx", split_axis=0, concat_axis=0, tiled=True)
        total, high, low = gram_step(rows.reshape(groups, steps, xlocal, zlocal), total)
        halves.append((high, low))
    gram = assemble(total_sum(total), order // BLOCK)
    basis = orthonormal(gram[:, :RANK])
    for step in range(ITERS):
        basis = orthonormal(product(gram, basis))
    mine = lax.dynamic_slice_in_dim(basis, lax.axis_index("gx") * xlocal, xlocal, 0)
    turned = basis.T
    keep = RANK // groups
    outs = []
    for high, low in halves:
        part = core_step(turned, high, low, zlocal).reshape(groups, keep, steps, zlocal)
        back = lax.all_to_all(part, "gx", split_axis=0, concat_axis=0, tiled=True)
        outs.append(jnp.swapaxes(back, 0, 1).reshape(keep, wide, zlocal))
    return (mine, jnp.concatenate(outs, axis=1))


def solution(mesh):
    in_specs = (P("gx", "gy", "gz"),)
    out_specs = (P("gx", None), P("gx", "gy", "gz"))
    return jax.shard_map(local, mesh=mesh, in_specs=in_specs, out_specs=out_specs, check_vma=False)
```

```python
import functools

import jax
import jax.numpy as jnp
from jax import lax
from jax.experimental import pallas as pl
from jax.experimental.pallas import tpu as pltpu
from jax.sharding import PartitionSpec as P

RANK = 128
ITERS = 2
BLOCK = 128
SUB = 8
AXES = ("gx", "gy", "gz")
VMEM = pl.BlockSpec(memory_space=pltpu.VMEM)
SMEM = pl.BlockSpec(memory_space=pltpu.SMEM)
ANY = pl.BlockSpec(memory_space=pl.ANY)
PARAMS = pltpu.CompilerParams(vmem_limit_bytes=20 * 2**20)


def product(left, right, contract=((1,), (0,))):
    return lax.dot_general(
        left, right, (contract, ((), ())), precision=lax.Precision.HIGHEST, preferred_element_type=jnp.float32
    )


def split(value):
    high = value.astype(jnp.bfloat16)
    low = (value - high.astype(jnp.float32)).astype(jnp.bfloat16)
    return high, low


def dot(left, right, contract):
    return lax.dot_general(left, right, (contract, ((), ())), preferred_element_type=jnp.float32)


def pack_kernel(groups, start, per, steps, me_ref, snapshot_ref, *refs):
    outs, held, sems = refs[:groups], refs[groups], refs[groups + 1]
    copies = []
    for shift in [*range(1, groups), 0]:
        owner = lax.rem(me_ref[0] + shift, groups)
        first = pl.multiple_of(owner * per + start, SUB)
        copy = pltpu.make_async_copy(snapshot_ref.at[:, pl.ds(first, steps), :], held.at[shift], sems.at[shift])
        copy.start()
        copies.append((shift, copy))
    for shift, copy in copies:
        copy.wait()
        for step in range(steps):
            outs[shift][step] = held[shift, :, step, :]


def pack(me, snapshot, groups, start, steps):
    xlocal, ylocal, zlocal = snapshot.shape
    per = ylocal // groups
    shape = (steps, xlocal, zlocal)
    if steps % SUB or per % SUB:
        parts = []
        for shift in range(groups):
            first = lax.rem(me[0] + shift, groups) * per + start
            parts.append(jnp.swapaxes(lax.dynamic_slice_in_dim(snapshot, first, steps, 1), 0, 1))
        return parts
    return pl.pallas_call(
        functools.partial(pack_kernel, groups, start, per, steps),
        out_shape=(jax.ShapeDtypeStruct(shape, jnp.float32),) * groups,
        in_specs=[SMEM, ANY],
        out_specs=(VMEM,) * groups,
        scratch_shapes=[
            pltpu.VMEM((groups, xlocal, steps, zlocal), jnp.float32),
            pltpu.SemaphoreType.DMA((groups,)),
        ],
        compiler_params=PARAMS,
        cost_estimate=pl.CostEstimate(flops=0, bytes_accessed=8 * groups * steps * xlocal * zlocal, transcendentals=0),
    )(me, snapshot)


def gram_kernel(first, groups, steps, xlocal, zlocal, me_ref, *refs):
    parts, refs = refs[:groups], refs[groups:]
    old_ref, (out_ref, high_ref, low_ref) = (None, refs) if first else (refs[0], refs[1:])
    for shift in range(groups):
        owner = lax.rem(me_ref[0] + groups - shift, groups)
        rows = pl.ds(pl.multiple_of(owner * xlocal, xlocal), xlocal)
        for step in range(steps):
            high, low = split(parts[shift][step])
            columns = slice(step * zlocal, (step + 1) * zlocal)
            high_ref[rows, columns] = high
            low_ref[rows, columns] = low
    order = groups * xlocal
    big = 2 * BLOCK if order % (2 * BLOCK) == 0 else BLOCK
    ratio = big // BLOCK
    last = ((1,), (1,))
    for row in range(order // big):
        left = slice(row * big, (row + 1) * big)
        for column in range(row + 1):
            right = slice(column * big, (column + 1) * big)
            total = dot(high_ref[left, :], high_ref[right, :], last)
            total += dot(high_ref[left, :], low_ref[right, :], last)
            total += dot(low_ref[left, :], high_ref[right, :], last)
            for i in range(ratio):
                for j in range(ratio):
                    r, c = row * ratio + i, column * ratio + j
                    if r < c:
                        continue
                    at = pl.ds((r * (r + 1) // 2 + c) * BLOCK, BLOCK)
                    block = total[i * BLOCK : (i + 1) * BLOCK, j * BLOCK : (j + 1) * BLOCK]
                    out_ref[at, :] = block if first else block + old_ref[at, :]


def gram_step(me, parts, old):
    groups = len(parts)
    steps, xlocal, zlocal = parts[0].shape
    order = groups * xlocal
    count = order // BLOCK
    first = old is None
    half = jax.ShapeDtypeStruct((order, steps * zlocal), jnp.bfloat16)
    operands = (me, *parts) if first else (me, *parts, old)
    return pl.pallas_call(
        functools.partial(gram_kernel, first, groups, steps, xlocal, zlocal),
        out_shape=(jax.ShapeDtypeStruct((count * (count + 1) // 2 * BLOCK, BLOCK), jnp.float32), half, half),
        in_specs=[SMEM] + [VMEM] * (len(operands) - 1),
        out_specs=(VMEM,) * 3,
        compiler_params=PARAMS,
        cost_estimate=pl.CostEstimate(
            flops=6 * order * order * steps * zlocal, bytes_accessed=8 * order * steps * zlocal, transcendentals=0
        ),
    )(*operands)


def inverse_cholesky(a_ref, b_ref, w_ref):
    order = a_ref.shape[0]
    wide = (SUB, order)
    below = lax.broadcasted_iota(jnp.int32, wide, 0)
    across = lax.broadcasted_iota(jnp.int32, wide, 1)
    for group in range(order // SUB):
        b_ref[group * SUB : (group + 1) * SUB, :] = jnp.where(across == below + group * SUB, 1.0, 0.0)

    def spread_row(value, row):
        return jnp.broadcast_to(value[row : row + 1, :], wide)

    for panel in range(order // SUB):
        at = slice(panel * SUB, (panel + 1) * SUB)
        a, b = a_ref[at, :], b_ref[at, :]
        columns = [jnp.broadcast_to(a[:, panel * SUB + k : panel * SUB + k + 1], wide) for k in range(SUB)]
        inverses, factors, scale = [], {}, jnp.zeros(wide, jnp.float32)
        for j in range(SUB):
            pivot = spread_row(columns[j], j)
            inverse = 1.0 / pivot
            inverses.append(inverse)
            scale = jnp.where(below == j, lax.rsqrt(pivot), scale)
            lower = jnp.where(below > j, columns[j], 0.0)
            for k in range(j + 1, SUB):
                factors[j, k] = spread_row(columns[k], j) * inverse
                columns[k] = columns[k] - lower * factors[j, k]
            lower = lower * inverse
            a = a - lower * spread_row(a, j)
            b = b - lower * spread_row(b, j)
        w_ref[at, :] = b * scale
        a_rows = [spread_row(a, j) * inverses[j] for j in range(SUB)]
        b_rows = [spread_row(b, j) * inverses[j] for j in range(SUB)]
        for group in range(panel + 1, order // SUB):
            rows = slice(group * SUB, (group + 1) * SUB)
            a, b = a_ref[rows, :], b_ref[rows, :]
            columns = [jnp.broadcast_to(a[:, panel * SUB + k : panel * SUB + k + 1], wide) for k in range(SUB)]
            for j in range(SUB):
                for k in range(j + 1, SUB):
                    columns[k] = columns[k] - columns[j] * factors[j, k]
                a = a - columns[j] * a_rows[j]
                b = b - columns[j] * b_rows[j]
            a_ref[rows, :] = a
            b_ref[rows, :] = b


def factor_kernel(order, xlocal, me_ref, blocks_ref, mine_ref, turned_ref, gram_ref, m_ref, a_ref, b_ref, w_ref):
    count = order // BLOCK
    for row in range(count):
        for column in range(row + 1):
            at = (row * (row + 1) // 2 + column) * BLOCK
            block = blocks_ref[at : at + BLOCK, :]
            gram_ref[row * BLOCK : (row + 1) * BLOCK, column * BLOCK : (column + 1) * BLOCK] = block
            if row != column:
                gram_ref[column * BLOCK : (column + 1) * BLOCK, row * BLOCK : (row + 1) * BLOCK] = block.T
    m_ref[...] = gram_ref[:, :RANK]

    def orthonormal():
        m = m_ref[...]
        a_ref[...] = product(m, m, ((0,), (0,)))
        inverse_cholesky(a_ref, b_ref, w_ref)
        return product(m, w_ref[...], ((1,), (1,)))

    def step(index, carry):
        basis = orthonormal()
        m_ref[...] = basis

        @pl.when(index < ITERS)
        def _():
            m_ref[...] = product(gram_ref[...], basis)

        return carry

    lax.fori_loop(0, ITERS + 1, step, 0)
    mine_ref[...] = m_ref[pl.ds(pl.multiple_of(me_ref[0] * xlocal, SUB), xlocal), :]
    turned_ref[...] = m_ref[...].T


def factor_step(me, blocks, order, xlocal):
    square = pltpu.VMEM((RANK, RANK), jnp.float32)
    return pl.pallas_call(
        functools.partial(factor_kernel, order, xlocal),
        out_shape=(
            jax.ShapeDtypeStruct((xlocal, RANK), jnp.float32),
            jax.ShapeDtypeStruct((RANK, order), jnp.float32),
        ),
        in_specs=[SMEM, VMEM],
        out_specs=(VMEM, VMEM),
        scratch_shapes=[
            pltpu.VMEM((order, order), jnp.float32),
            pltpu.VMEM((order, RANK), jnp.float32),
            square,
            square,
            square,
        ],
        compiler_params=PARAMS,
    )(me, blocks)


def core_kernel(groups, keep, steps, zlocal, me_ref, turned_ref, high_ref, low_ref, *outs):
    lines = []
    for shift in range(groups):
        owner = lax.rem(me_ref[0] + shift, groups)
        lines.append(turned_ref[pl.ds(pl.multiple_of(owner * keep, SUB), keep), :])
    high, low = split(jnp.concatenate(lines, axis=0))
    natural = ((1,), (0,))
    total = dot(high, high_ref[...], natural) + dot(high, low_ref[...], natural) + dot(low, high_ref[...], natural)
    for shift in range(groups):
        for step in range(steps):
            outs[shift][:, step, :] = total[shift * keep : (shift + 1) * keep, step * zlocal : (step + 1) * zlocal]


def core_step(me, turned, high, low, groups, zlocal):
    order, width = high.shape
    steps = width // zlocal
    keep = RANK // groups
    return pl.pallas_call(
        functools.partial(core_kernel, groups, keep, steps, zlocal),
        out_shape=(jax.ShapeDtypeStruct((keep, steps, zlocal), jnp.float32),) * groups,
        in_specs=[SMEM] + [VMEM] * 3,
        out_specs=(VMEM,) * groups,
        compiler_params=PARAMS,
        cost_estimate=pl.CostEstimate(flops=6 * RANK * order * width, bytes_accessed=6 * order * width, transcendentals=0),
    )(me, turned, high, low)


def place_kernel(groups, per, starts, steps, me_ref, *refs):
    parts, out_ref, sem = refs[:-2], refs[-2], refs[-1]
    copies = []
    for chunk, start in enumerate(starts):
        for shift in range(groups):
            owner = lax.rem(me_ref[0] + groups - shift, groups)
            first = pl.multiple_of(owner * per + start, SUB)
            index = chunk * groups + shift
            copy = pltpu.make_async_copy(parts[index], out_ref.at[:, pl.ds(first, steps), :], sem.at[index])
            copy.start()
            copies.append(copy)
    for copy in copies:
        copy.wait()


def place(me, chunks, starts, ylocal):
    groups = len(chunks[0])
    keep, steps, zlocal = chunks[0][0].shape
    per = ylocal // groups
    shape = (keep, ylocal, zlocal)
    if steps % SUB or per % SUB:
        out = jnp.zeros(shape, jnp.float32)
        for start, parts in zip(starts, chunks):
            for shift, part in enumerate(parts):
                first = lax.rem(me[0] + groups - shift, groups) * per + start
                out = lax.dynamic_update_slice_in_dim(out, part, first, 1)
        return out
    parts = [part for parts in chunks for part in parts]
    return pl.pallas_call(
        functools.partial(place_kernel, groups, per, starts, steps),
        out_shape=jax.ShapeDtypeStruct(shape, jnp.float32),
        in_specs=[SMEM] + [ANY] * len(parts),
        out_specs=ANY,
        scratch_shapes=[pltpu.SemaphoreType.DMA((len(parts),))],
        compiler_params=PARAMS,
    )(me, *parts)


def exchange(parts):
    groups = len(parts)
    moved = [parts[0]]
    for shift in range(1, groups):
        moved.append(lax.ppermute(parts[shift], "gx", [(i, (i + shift) % groups) for i in range(groups)]))
    return moved


def total_sum(blocks):
    devices = lax.axis_size(AXES)
    rows = blocks.shape[0]
    share = -(-rows // devices)
    flat = jnp.pad(blocks, ((0, share * devices - rows), (0, 0)))
    parts = lax.all_to_all(flat.reshape(devices, share, BLOCK), AXES, split_axis=0, concat_axis=0, tiled=True)
    mine = jnp.sum(parts, axis=0)
    spread = jnp.broadcast_to(mine[None], (devices, share, BLOCK))
    whole = lax.all_to_all(spread, AXES, split_axis=0, concat_axis=0, tiled=True)
    return whole.reshape(-1, BLOCK)


def chunk_count(per):
    return max(k for k in range(1, 6) if per % k == 0)


def local(snapshot):
    xlocal, ylocal, zlocal = snapshot.shape
    groups = lax.axis_size("gx")
    order = groups * xlocal
    per = ylocal // groups
    chunks = chunk_count(per)
    steps = per // chunks
    starts = [chunk * steps for chunk in range(chunks)]
    me = lax.axis_index("gx").astype(jnp.int32).reshape(1)
    halves = []
    total = None
    for start in starts:
        total, high, low = gram_step(me, exchange(pack(me, snapshot, groups, start, steps)), total)
        halves.append((high, low))
    mine, turned = factor_step(me, total_sum(total), order, xlocal)
    outs = [exchange(core_step(me, turned, high, low, groups, zlocal)) for high, low in halves]
    return (mine, place(me, outs, starts, ylocal))


def solution(mesh):
    in_specs = (P("gx", "gy", "gz"),)
    out_specs = (P("gx", None), P("gx", "gy", "gz"))
    return jax.shard_map(local, mesh=mesh, in_specs=in_specs, out_specs=out_specs, check_vma=False)
```

```python
import functools

import jax
import jax.numpy as jnp
from jax import lax
from jax.experimental import pallas as pl
from jax.experimental.pallas import tpu as pltpu
from jax.sharding import PartitionSpec as P

RANK = 128
ITERS = 2
BLOCK = 128
SUB = 8
HALF = 16
AXES = ("gx", "gy", "gz")
VMEM = pl.BlockSpec(memory_space=pltpu.VMEM)
SMEM = pl.BlockSpec(memory_space=pltpu.SMEM)
ANY = pl.BlockSpec(memory_space=pl.ANY)
HBM = pl.BlockSpec(memory_space=pltpu.HBM)
PARAMS = pltpu.CompilerParams(vmem_limit_bytes=12 * 2**20)


def product(left, right, contract=((1,), (0,))):
    return lax.dot_general(
        left, right, (contract, ((), ())), precision=lax.Precision.HIGHEST, preferred_element_type=jnp.float32
    )


def split(value):
    high = value.astype(jnp.bfloat16)
    low = (value - high.astype(jnp.float32)).astype(jnp.bfloat16)
    return high, low


def dot(left, right, contract):
    return lax.dot_general(left, right, (contract, ((), ())), preferred_element_type=jnp.float32)


def pack_kernel(groups, x0, tall, start, per, steps, me_ref, snapshot_ref, *refs):
    outs, held, sems = refs[:groups], refs[groups], refs[groups + 1]
    copies = []
    for shift in [*range(1, groups), 0]:
        owner = lax.rem(me_ref[0] + shift, groups)
        first = pl.multiple_of(owner * per + start, SUB)
        source = snapshot_ref.at[pl.ds(x0, tall), pl.ds(first, steps), :]
        copy = pltpu.make_async_copy(source, held.at[shift], sems.at[shift])
        copy.start()
        copies.append((shift, copy))
    for shift, copy in copies:
        copy.wait()
        for step in range(steps):
            outs[shift][step] = held[shift, :, step, :]


def pack(me, snapshot, groups, x0, tall, start, steps):
    _, ylocal, zlocal = snapshot.shape
    per = ylocal // groups
    shape = (steps, tall, zlocal)
    if steps % SUB or per % SUB:
        parts = []
        for shift in range(groups):
            first = lax.rem(me[0] + shift, groups) * per + start
            piece = lax.dynamic_slice_in_dim(snapshot[x0 : x0 + tall], first, steps, 1)
            parts.append(jnp.swapaxes(piece, 0, 1))
        return parts
    return pl.pallas_call(
        functools.partial(pack_kernel, groups, x0, tall, start, per, steps),
        out_shape=(jax.ShapeDtypeStruct(shape, jnp.float32),) * groups,
        in_specs=[SMEM, HBM],
        out_specs=(VMEM,) * groups,
        scratch_shapes=[
            pltpu.VMEM((groups, tall, steps, zlocal), jnp.float32),
            pltpu.SemaphoreType.DMA((groups,)),
        ],
        compiler_params=PARAMS,
        cost_estimate=pl.CostEstimate(flops=0, bytes_accessed=8 * groups * steps * tall * zlocal, transcendentals=0),
    )(me, snapshot)


def gram_kernel(first, groups, earlier, me_ref, *refs):
    parts, refs = refs[:groups], refs[groups:]
    highs, lows, refs = list(refs[:earlier]), list(refs[earlier : 2 * earlier]), refs[2 * earlier :]
    old_ref, (out_ref, high_ref, low_ref) = (None, refs) if first else (refs[0], refs[1:])
    steps, tall, zlocal = parts[0].shape
    for shift in range(groups):
        owner = lax.rem(me_ref[0] + groups - shift, groups)
        rows = pl.ds(pl.multiple_of(owner * tall, HALF), tall)
        for step in range(steps):
            high, low = split(parts[shift][step])
            columns = slice(step * zlocal, (step + 1) * zlocal)
            high_ref[rows, columns] = high
            low_ref[rows, columns] = low
    last = ((1,), (1,))
    slot = 0
    for row in range(groups * tall // BLOCK):
        mine = slice(row * BLOCK, (row + 1) * BLOCK)
        for other_high, other_low in [*zip(highs, lows), (high_ref, low_ref)]:
            upto = slice(0, (row + 1) * BLOCK if other_high is high_ref else other_high.shape[0])
            total = dot(high_ref[mine, :], other_high[upto, :], last)
            total += dot(high_ref[mine, :], other_low[upto, :], last)
            total += dot(low_ref[mine, :], other_high[upto, :], last)
            for column in range(upto.stop // BLOCK):
                at = slice(slot * BLOCK, (slot + 1) * BLOCK)
                block = total[:, column * BLOCK : (column + 1) * BLOCK]
                out_ref[at, :] = block if first else block + old_ref[at, :]
                slot += 1


def gram_step(me, parts, earlier, old):
    groups = len(parts)
    steps, tall, zlocal = parts[0].shape
    rows = groups * tall
    before = sum(high.shape[0] for high, _ in earlier)
    done, count = before // BLOCK, rows // BLOCK
    slots = done * count + count * (count + 1) // 2
    first = old is None
    half = jax.ShapeDtypeStruct((rows, steps * zlocal), jnp.bfloat16)
    operands = [me, *parts, *(high for high, _ in earlier), *(low for _, low in earlier)]
    operands += [] if first else [old]
    return pl.pallas_call(
        functools.partial(gram_kernel, first, groups, len(earlier)),
        out_shape=(jax.ShapeDtypeStruct((slots * BLOCK, BLOCK), jnp.float32), half, half),
        in_specs=[SMEM] + [VMEM] * (len(operands) - 1),
        out_specs=(VMEM,) * 3,
        compiler_params=PARAMS,
        cost_estimate=pl.CostEstimate(
            flops=6 * slots * BLOCK * BLOCK * steps * zlocal, bytes_accessed=8 * rows * steps * zlocal, transcendentals=0
        ),
    )(*operands)


def inverse_cholesky(a_ref, b_ref, w_ref):
    order = a_ref.shape[0]
    wide = (SUB, order)
    below = lax.broadcasted_iota(jnp.int32, wide, 0)
    across = lax.broadcasted_iota(jnp.int32, wide, 1)
    for group in range(order // SUB):
        b_ref[group * SUB : (group + 1) * SUB, :] = jnp.where(across == below + group * SUB, 1.0, 0.0)

    def spread_row(value, row):
        return jnp.broadcast_to(value[row : row + 1, :], wide)

    for panel in range(order // SUB):
        at = slice(panel * SUB, (panel + 1) * SUB)
        a, b = a_ref[at, :], b_ref[at, :]
        columns = [jnp.broadcast_to(a[:, panel * SUB + k : panel * SUB + k + 1], wide) for k in range(SUB)]
        inverses, factors, scale = [], {}, jnp.zeros(wide, jnp.float32)
        for j in range(SUB):
            pivot = spread_row(columns[j], j)
            inverse = 1.0 / pivot
            inverses.append(inverse)
            scale = jnp.where(below == j, lax.rsqrt(pivot), scale)
            lower = jnp.where(below > j, columns[j], 0.0)
            for k in range(j + 1, SUB):
                factors[j, k] = spread_row(columns[k], j) * inverse
                columns[k] = columns[k] - lower * factors[j, k]
            lower = lower * inverse
            a = a - lower * spread_row(a, j)
            b = b - lower * spread_row(b, j)
        w_ref[at, :] = b * scale
        a_rows = [spread_row(a, j) * inverses[j] for j in range(SUB)]
        b_rows = [spread_row(b, j) * inverses[j] for j in range(SUB)]
        for group in range(panel + 1, order // SUB):
            rows = slice(group * SUB, (group + 1) * SUB)
            a, b = a_ref[rows, :], b_ref[rows, :]
            columns = [jnp.broadcast_to(a[:, panel * SUB + k : panel * SUB + k + 1], wide) for k in range(SUB)]
            for j in range(SUB):
                for k in range(j + 1, SUB):
                    columns[k] = columns[k] - columns[j] * factors[j, k]
                a = a - columns[j] * a_rows[j]
                b = b - columns[j] * b_rows[j]
            a_ref[rows, :] = a
            b_ref[rows, :] = b


def factor_kernel(groups, talls, me_ref, *refs):
    phases = len(talls)
    sums, refs = refs[:phases], refs[phases:]
    mine_ref, turned_ref, gram_ref, m_ref, a_ref, b_ref, w_ref = refs
    bases = [groups * sum(talls[:phase]) for phase in range(phases)]
    xlocal = sum(talls)
    for phase, tall in enumerate(talls):
        slot = 0
        first = bases[phase] // BLOCK
        for row in range(first, first + groups * tall // BLOCK):
            for column in range(row + 1):
                block = sums[phase][slot * BLOCK : (slot + 1) * BLOCK, :]
                slot += 1
                gram_ref[row * BLOCK : (row + 1) * BLOCK, column * BLOCK : (column + 1) * BLOCK] = block
                if row != column:
                    gram_ref[column * BLOCK : (column + 1) * BLOCK, row * BLOCK : (row + 1) * BLOCK] = block.T
    lines = []
    for owner in range(-(-RANK // xlocal)):
        for base, tall in zip(bases, talls):
            lines.append(gram_ref[base + owner * tall : base + (owner + 1) * tall, :])
    m_ref[...] = jnp.concatenate(lines, axis=0)[:RANK, :].T

    def step(index, carry):
        m = m_ref[...]
        a_ref[...] = product(m, m, ((0,), (0,)))
        inverse_cholesky(a_ref, b_ref, w_ref)
        basis = product(m, w_ref[...], ((1,), (1,)))
        m_ref[...] = basis

        @pl.when(index < ITERS)
        def _():
            m_ref[...] = product(gram_ref[...], basis)

        return carry

    lax.fori_loop(0, ITERS + 1, step, 0)
    offset = 0
    for base, tall in zip(bases, talls):
        rows = pl.ds(pl.multiple_of(base + me_ref[0] * tall, SUB), tall)
        mine_ref[offset : offset + tall, :] = m_ref[rows, :]
        offset += tall
    turned_ref[...] = m_ref[...].T


def factor_step(me, sums, groups, talls):
    order, xlocal = groups * sum(talls), sum(talls)
    square = pltpu.VMEM((RANK, RANK), jnp.float32)
    return pl.pallas_call(
        functools.partial(factor_kernel, groups, talls),
        out_shape=(
            jax.ShapeDtypeStruct((xlocal, RANK), jnp.float32),
            jax.ShapeDtypeStruct((RANK, order), jnp.float32),
        ),
        in_specs=[SMEM] + [VMEM] * len(sums),
        out_specs=(VMEM, VMEM),
        scratch_shapes=[
            pltpu.VMEM((order, order), jnp.float32),
            pltpu.VMEM((order, RANK), jnp.float32),
            square,
            square,
            square,
        ],
        compiler_params=PARAMS,
    )(me, *sums)


def core_kernel(groups, keep, steps, zlocal, phases, me_ref, turned_ref, *refs):
    highs, lows, outs = refs[:phases], refs[phases : 2 * phases], refs[2 * phases :]
    lines = []
    for shift in range(groups):
        owner = lax.rem(me_ref[0] + shift, groups)
        lines.append(turned_ref[pl.ds(pl.multiple_of(owner * keep, SUB), keep), :])
    high, low = split(jnp.concatenate(lines, axis=0))
    natural = ((1,), (0,))
    total, base = 0.0, 0
    for high_ref, low_ref in zip(highs, lows):
        rows = slice(base, base + high_ref.shape[0])
        base = rows.stop
        total += dot(high[:, rows], high_ref[...], natural)
        total += dot(high[:, rows], low_ref[...], natural)
        total += dot(low[:, rows], high_ref[...], natural)
    for shift in range(groups):
        for step in range(steps):
            outs[shift][:, step, :] = total[shift * keep : (shift + 1) * keep, step * zlocal : (step + 1) * zlocal]


def core_step(me, turned, halves, groups, zlocal):
    order, width = turned.shape[1], halves[0][0].shape[1]
    steps = width // zlocal
    keep = RANK // groups
    return pl.pallas_call(
        functools.partial(core_kernel, groups, keep, steps, zlocal, len(halves)),
        out_shape=(jax.ShapeDtypeStruct((keep, steps, zlocal), jnp.float32),) * groups,
        in_specs=[SMEM] + [VMEM] * (1 + 2 * len(halves)),
        out_specs=(VMEM,) * groups,
        compiler_params=PARAMS,
        cost_estimate=pl.CostEstimate(flops=6 * RANK * order * width, bytes_accessed=6 * order * width, transcendentals=0),
    )(me, turned, *(high for high, _ in halves), *(low for _, low in halves))


def place_kernel(groups, per, starts, steps, me_ref, *refs):
    parts, out_ref, sem = refs[:-2], refs[-2], refs[-1]
    copies = []
    for chunk, start in enumerate(starts):
        for shift in range(groups):
            owner = lax.rem(me_ref[0] + groups - shift, groups)
            first = pl.multiple_of(owner * per + start, SUB)
            index = chunk * groups + shift
            copy = pltpu.make_async_copy(parts[index], out_ref.at[:, pl.ds(first, steps), :], sem.at[index])
            copy.start()
            copies.append(copy)
    for copy in copies:
        copy.wait()


def place(me, chunks, starts, ylocal):
    groups = len(chunks[0])
    keep, steps, zlocal = chunks[0][0].shape
    per = ylocal // groups
    shape = (keep, ylocal, zlocal)
    if steps % SUB or per % SUB:
        out = jnp.zeros(shape, jnp.float32)
        for start, parts in zip(starts, chunks):
            for shift, part in enumerate(parts):
                first = lax.rem(me[0] + groups - shift, groups) * per + start
                out = lax.dynamic_update_slice_in_dim(out, part, first, 1)
        return out
    parts = [part for parts in chunks for part in parts]
    return pl.pallas_call(
        functools.partial(place_kernel, groups, per, starts, steps),
        out_shape=jax.ShapeDtypeStruct(shape, jnp.float32),
        in_specs=[SMEM] + [ANY] * len(parts),
        out_specs=ANY,
        scratch_shapes=[pltpu.SemaphoreType.DMA((len(parts),))],
        compiler_params=PARAMS,
    )(me, *parts)


def exchange(parts):
    groups = len(parts)
    moved = [parts[0]]
    for shift in range(1, groups):
        moved.append(lax.ppermute(parts[shift], "gx", [(i, (i + shift) % groups) for i in range(groups)]))
    return moved


def total_sum(blocks):
    devices = lax.axis_size(AXES)
    rows = blocks.shape[0]
    share = -(-rows // devices)
    flat = jnp.pad(blocks, ((0, share * devices - rows), (0, 0)))
    parts = lax.all_to_all(flat.reshape(devices, share, BLOCK), AXES, split_axis=0, concat_axis=0, tiled=True)
    mine = jnp.sum(parts, axis=0)
    spread = jnp.broadcast_to(mine[None], (devices, share, BLOCK))
    whole = lax.all_to_all(spread, AXES, split_axis=0, concat_axis=0, tiled=True)
    return whole.reshape(-1, BLOCK)


def chunk_count(per):
    return max(k for k in range(1, 6) if per % k == 0)


def phase_sizes(xlocal, groups):
    short = xlocal // 4
    if short % HALF or groups * short % BLOCK:
        short = xlocal // 2
    return [xlocal - short, short]


def local(snapshot):
    xlocal, ylocal, zlocal = snapshot.shape
    groups = lax.axis_size("gx")
    per = ylocal // groups
    chunks = chunk_count(per)
    steps = per // chunks
    starts = [chunk * steps for chunk in range(chunks)]
    talls = phase_sizes(xlocal, groups)
    me = lax.axis_index("gx").astype(jnp.int32).reshape(1)
    halves = [[] for _ in starts]
    sums = []
    x0 = 0
    for tall in talls:
        total = None
        for held, start in zip(halves, starts):
            parts = exchange(pack(me, snapshot, groups, x0, tall, start, steps))
            total, high, low = gram_step(me, parts, held, total)
            held.append((high, low))
        x0 += tall
        sums.append(total_sum(total) if x0 == xlocal else lax.psum(total, AXES))
    mine, turned = factor_step(me, sums, groups, talls)
    outs = [exchange(core_step(me, turned, held, groups, zlocal)) for held in halves]
    return (mine, place(me, outs, starts, ylocal))


def solution(mesh):
    in_specs = (P("gx", "gy", "gz"),)
    out_specs = (P("gx", None), P("gx", "gy", "gz"))
    return jax.shard_map(local, mesh=mesh, in_specs=in_specs, out_specs=out_specs, check_vma=False)
```

```python
import functools

import jax
import jax.numpy as jnp
from jax import lax
from jax.experimental import pallas as pl
from jax.experimental.pallas import tpu as pltpu
from jax.sharding import PartitionSpec as P

RANK = 128
ITERS = 2
BLOCK = 128
SUB = 8
HALF = 16
AXES = ("gx", "gy", "gz")
VMEM = pl.BlockSpec(memory_space=pltpu.VMEM)
SMEM = pl.BlockSpec(memory_space=pltpu.SMEM)
ANY = pl.BlockSpec(memory_space=pl.ANY)
HBM = pl.BlockSpec(memory_space=pltpu.HBM)
PARAMS = pltpu.CompilerParams(vmem_limit_bytes=12 * 2**20)


def product(left, right, contract=((1,), (0,))):
    return lax.dot_general(
        left, right, (contract, ((), ())), precision=lax.Precision.HIGHEST, preferred_element_type=jnp.float32
    )


def split(value):
    high = value.astype(jnp.bfloat16)
    low = (value - high.astype(jnp.float32)).astype(jnp.bfloat16)
    return high, low


def dot(left, right, contract):
    return lax.dot_general(left, right, (contract, ((), ())), preferred_element_type=jnp.float32)


def pack_kernel(groups, per, pieces, me_ref, snapshot_ref, *refs):
    outs, refs = refs[: groups * len(pieces)], refs[groups * len(pieces) :]
    helds, sems = refs[:-1], refs[-1]
    copies = []
    for index, (x0, tall, start, steps) in enumerate(pieces):
        for shift in [*range(1, groups), 0]:
            owner = lax.rem(me_ref[0] + shift, groups)
            first = pl.multiple_of(owner * per + start, SUB)
            source = snapshot_ref.at[pl.ds(x0, tall), pl.ds(first, steps), :]
            copy = pltpu.make_async_copy(source, helds[index].at[shift], sems.at[index * groups + shift])
            copy.start()
            copies.append((index, shift, copy))
    for index, shift, copy in copies:
        copy.wait()
        for step in range(pieces[index][3]):
            outs[index * groups + shift][step] = helds[index][shift, :, step, :]


def pack(me, snapshot, groups, pieces, limit):
    _, ylocal, zlocal = snapshot.shape
    per = ylocal // groups
    if per % SUB or any(steps % SUB for _, _, _, steps in pieces):
        parts = []
        for x0, tall, start, steps in pieces:
            for shift in range(groups):
                first = lax.rem(me[0] + shift, groups) * per + start
                piece = lax.dynamic_slice_in_dim(snapshot[x0 : x0 + tall], first, steps, 1)
                parts.append(jnp.swapaxes(piece, 0, 1))
    else:
        outs, helds = [], []
        for _, tall, _, steps in pieces:
            outs += [jax.ShapeDtypeStruct((steps, tall, zlocal), jnp.float32)] * groups
            helds.append(pltpu.VMEM((groups, tall, steps, zlocal), jnp.float32))
        parts = pl.pallas_call(
            functools.partial(pack_kernel, groups, per, tuple(pieces)),
            out_shape=tuple(outs),
            in_specs=[SMEM, HBM],
            out_specs=(VMEM,) * len(outs),
            scratch_shapes=[*helds, pltpu.SemaphoreType.DMA((len(outs),))],
            compiler_params=pltpu.CompilerParams(vmem_limit_bytes=limit),
            cost_estimate=pl.CostEstimate(
                flops=0, bytes_accessed=8 * sum(groups * tall * steps * zlocal for _, tall, _, steps in pieces), transcendentals=0
            ),
        )(me, snapshot)
    return [list(parts[at : at + groups]) for at in range(0, len(parts), groups)]


def gram_kernel(first, groups, chunks, earlier, me_ref, *refs):
    parts, refs = refs[:groups], refs[groups:]
    held, refs = refs[: 2 * chunks * earlier], refs[2 * chunks * earlier :]
    old_ref, refs = (None, refs) if first else (refs[0], refs[1:])
    out_ref, made = refs[0], refs[1:]
    wide, tall, zlocal = parts[0].shape
    steps = wide // chunks
    last = ((1,), (1,))
    for chunk in range(chunks):
        high_ref, low_ref = made[2 * chunk : 2 * chunk + 2]
        for shift in range(groups):
            owner = lax.rem(me_ref[0] + groups - shift, groups)
            rows = pl.ds(pl.multiple_of(owner * tall, HALF), tall)
            for step in range(steps):
                high, low = split(parts[shift][chunk * steps + step])
                columns = slice(step * zlocal, (step + 1) * zlocal)
                high_ref[rows, columns] = high
                low_ref[rows, columns] = low
        pairs = held[2 * chunk * earlier : 2 * (chunk + 1) * earlier]
        pairs = [*zip(pairs[::2], pairs[1::2]), (high_ref, low_ref)]
        slot = 0
        for row in range(groups * tall // BLOCK):
            mine = slice(row * BLOCK, (row + 1) * BLOCK)
            for other_high, other_low in pairs:
                upto = slice(0, (row + 1) * BLOCK if other_high is high_ref else other_high.shape[0])
                total = dot(high_ref[mine, :], other_high[upto, :], last)
                total += dot(high_ref[mine, :], other_low[upto, :], last)
                total += dot(low_ref[mine, :], other_high[upto, :], last)
                for column in range(upto.stop // BLOCK):
                    at = slice(slot * BLOCK, (slot + 1) * BLOCK)
                    block = total[:, column * BLOCK : (column + 1) * BLOCK]
                    if chunk:
                        block += out_ref[at, :]
                    elif not first:
                        block += old_ref[at, :]
                    out_ref[at, :] = block
                    slot += 1


def gram_step(me, parts, earlier, old):
    groups, chunks = len(parts), len(earlier)
    wide, tall, zlocal = parts[0].shape
    rows = groups * tall
    before = sum(high.shape[0] for high, _ in earlier[0])
    done, count = before // BLOCK, rows // BLOCK
    slots = done * count + count * (count + 1) // 2
    first = old is None
    half = jax.ShapeDtypeStruct((rows, wide // chunks * zlocal), jnp.bfloat16)
    operands = [me, *parts, *(half for held in earlier for pair in held for half in pair)]
    operands += [] if first else [old]
    total, *made = pl.pallas_call(
        functools.partial(gram_kernel, first, groups, chunks, len(earlier[0])),
        out_shape=(jax.ShapeDtypeStruct((slots * BLOCK, BLOCK), jnp.float32),) + (half,) * (2 * chunks),
        in_specs=[SMEM] + [VMEM] * (len(operands) - 1),
        out_specs=(VMEM,) * (1 + 2 * chunks),
        compiler_params=PARAMS,
        cost_estimate=pl.CostEstimate(
            flops=6 * slots * BLOCK * BLOCK * wide * zlocal, bytes_accessed=8 * rows * wide * zlocal, transcendentals=0
        ),
    )(*operands)
    return total, list(zip(made[::2], made[1::2]))


def inverse_cholesky(a_ref, b_ref, w_ref):
    order = a_ref.shape[0]
    wide = (SUB, order)
    below = lax.broadcasted_iota(jnp.int32, wide, 0)
    across = lax.broadcasted_iota(jnp.int32, wide, 1)
    for group in range(order // SUB):
        b_ref[group * SUB : (group + 1) * SUB, :] = jnp.where(across == below + group * SUB, 1.0, 0.0)

    def spread_row(value, row):
        return jnp.broadcast_to(value[row : row + 1, :], wide)

    for panel in range(order // SUB):
        at = slice(panel * SUB, (panel + 1) * SUB)
        a, b = a_ref[at, :], b_ref[at, :]
        columns = [jnp.broadcast_to(a[:, panel * SUB + k : panel * SUB + k + 1], wide) for k in range(SUB)]
        inverses, factors, scale = [], {}, jnp.zeros(wide, jnp.float32)
        for j in range(SUB):
            pivot = spread_row(columns[j], j)
            inverse = 1.0 / pivot
            inverses.append(inverse)
            scale = jnp.where(below == j, lax.rsqrt(pivot), scale)
            lower = jnp.where(below > j, columns[j], 0.0)
            for k in range(j + 1, SUB):
                factors[j, k] = spread_row(columns[k], j) * inverse
                columns[k] = columns[k] - lower * factors[j, k]
            lower = lower * inverse
            a = a - lower * spread_row(a, j)
            b = b - lower * spread_row(b, j)
        w_ref[at, :] = b * scale
        a_rows = [spread_row(a, j) * inverses[j] for j in range(SUB)]
        b_rows = [spread_row(b, j) * inverses[j] for j in range(SUB)]
        for group in range(panel + 1, order // SUB):
            rows = slice(group * SUB, (group + 1) * SUB)
            a, b = a_ref[rows, :], b_ref[rows, :]
            columns = [jnp.broadcast_to(a[:, panel * SUB + k : panel * SUB + k + 1], wide) for k in range(SUB)]
            for j in range(SUB):
                for k in range(j + 1, SUB):
                    columns[k] = columns[k] - columns[j] * factors[j, k]
                a = a - columns[j] * a_rows[j]
                b = b - columns[j] * b_rows[j]
            a_ref[rows, :] = a
            b_ref[rows, :] = b


def factor_kernel(groups, talls, me_ref, *refs):
    phases = len(talls)
    sums, refs = refs[:phases], refs[phases:]
    mine_ref, turned_ref, gram_ref, m_ref, a_ref, b_ref, w_ref = refs
    bases = [groups * sum(talls[:phase]) for phase in range(phases)]
    xlocal = sum(talls)
    for phase, tall in enumerate(talls):
        slot = 0
        first = bases[phase] // BLOCK
        for row in range(first, first + groups * tall // BLOCK):
            for column in range(row + 1):
                block = sums[phase][slot * BLOCK : (slot + 1) * BLOCK, :]
                slot += 1
                gram_ref[row * BLOCK : (row + 1) * BLOCK, column * BLOCK : (column + 1) * BLOCK] = block
                if row != column:
                    gram_ref[column * BLOCK : (column + 1) * BLOCK, row * BLOCK : (row + 1) * BLOCK] = block.T
    lines = []
    for owner in range(-(-RANK // xlocal)):
        for base, tall in zip(bases, talls):
            lines.append(gram_ref[base + owner * tall : base + (owner + 1) * tall, :])
    m_ref[...] = jnp.concatenate(lines, axis=0)[:RANK, :].T

    def step(index, carry):
        m = m_ref[...]
        a_ref[...] = product(m, m, ((0,), (0,)))
        inverse_cholesky(a_ref, b_ref, w_ref)
        basis = product(m, w_ref[...], ((1,), (1,)))
        m_ref[...] = basis

        @pl.when(index < ITERS)
        def _():
            m_ref[...] = product(gram_ref[...], basis)

        return carry

    lax.fori_loop(0, ITERS + 1, step, 0)
    offset = 0
    for base, tall in zip(bases, talls):
        rows = pl.ds(pl.multiple_of(base + me_ref[0] * tall, SUB), tall)
        mine_ref[offset : offset + tall, :] = m_ref[rows, :]
        offset += tall
    turned_ref[...] = m_ref[...].T


def factor_step(me, sums, groups, talls):
    order, xlocal = groups * sum(talls), sum(talls)
    square = pltpu.VMEM((RANK, RANK), jnp.float32)
    return pl.pallas_call(
        functools.partial(factor_kernel, groups, talls),
        out_shape=(
            jax.ShapeDtypeStruct((xlocal, RANK), jnp.float32),
            jax.ShapeDtypeStruct((RANK, order), jnp.float32),
        ),
        in_specs=[SMEM] + [VMEM] * len(sums),
        out_specs=(VMEM, VMEM),
        scratch_shapes=[
            pltpu.VMEM((order, order), jnp.float32),
            pltpu.VMEM((order, RANK), jnp.float32),
            square,
            square,
            square,
        ],
        compiler_params=PARAMS,
    )(me, *sums)


def core_kernel(groups, keep, steps, zlocal, phases, me_ref, turned_ref, *refs):
    highs, lows, outs = refs[:phases], refs[phases : 2 * phases], refs[2 * phases :]
    lines = []
    for shift in range(groups):
        owner = lax.rem(me_ref[0] + shift, groups)
        lines.append(turned_ref[pl.ds(pl.multiple_of(owner * keep, SUB), keep), :])
    high, low = split(jnp.concatenate(lines, axis=0))
    natural = ((1,), (0,))
    total, base = 0.0, 0
    for high_ref, low_ref in zip(highs, lows):
        rows = slice(base, base + high_ref.shape[0])
        base = rows.stop
        total += dot(high[:, rows], high_ref[...], natural)
        total += dot(high[:, rows], low_ref[...], natural)
        total += dot(low[:, rows], high_ref[...], natural)
    for shift in range(groups):
        for step in range(steps):
            outs[shift][:, step, :] = total[shift * keep : (shift + 1) * keep, step * zlocal : (step + 1) * zlocal]


def core_step(me, turned, halves, groups, zlocal):
    order, width = turned.shape[1], halves[0][0].shape[1]
    steps = width // zlocal
    keep = RANK // groups
    return pl.pallas_call(
        functools.partial(core_kernel, groups, keep, steps, zlocal, len(halves)),
        out_shape=(jax.ShapeDtypeStruct((keep, steps, zlocal), jnp.float32),) * groups,
        in_specs=[SMEM] + [VMEM] * (1 + 2 * len(halves)),
        out_specs=(VMEM,) * groups,
        compiler_params=PARAMS,
        cost_estimate=pl.CostEstimate(flops=6 * RANK * order * width, bytes_accessed=6 * order * width, transcendentals=0),
    )(me, turned, *(high for high, _ in halves), *(low for _, low in halves))


def place_kernel(groups, per, starts, steps, me_ref, *refs):
    parts, out_ref, sem = refs[:-2], refs[-2], refs[-1]
    copies = []
    for chunk, start in enumerate(starts):
        for shift in range(groups):
            owner = lax.rem(me_ref[0] + groups - shift, groups)
            first = pl.multiple_of(owner * per + start, SUB)
            index = chunk * groups + shift
            copy = pltpu.make_async_copy(parts[index], out_ref.at[:, pl.ds(first, steps), :], sem.at[index])
            copy.start()
            copies.append(copy)
    for copy in copies:
        copy.wait()


def place(me, chunks, starts, ylocal):
    groups = len(chunks[0])
    keep, steps, zlocal = chunks[0][0].shape
    per = ylocal // groups
    shape = (keep, ylocal, zlocal)
    if steps % SUB or per % SUB:
        out = jnp.zeros(shape, jnp.float32)
        for start, parts in zip(starts, chunks):
            for shift, part in enumerate(parts):
                first = lax.rem(me[0] + groups - shift, groups) * per + start
                out = lax.dynamic_update_slice_in_dim(out, part, first, 1)
        return out
    parts = [part for parts in chunks for part in parts]
    return pl.pallas_call(
        functools.partial(place_kernel, groups, per, starts, steps),
        out_shape=jax.ShapeDtypeStruct(shape, jnp.float32),
        in_specs=[SMEM] + [ANY] * len(parts),
        out_specs=ANY,
        scratch_shapes=[pltpu.SemaphoreType.DMA((len(parts),))],
        compiler_params=PARAMS,
    )(me, *parts)


def exchange(parts):
    groups = len(parts)
    moved = [parts[0]]
    for shift in range(1, groups):
        moved.append(lax.ppermute(parts[shift], "gx", [(i, (i + shift) % groups) for i in range(groups)]))
    return moved


def total_sum(blocks, stages):
    rows = blocks.shape[0]
    flat = jnp.pad(blocks, ((0, -rows % lax.axis_size(AXES)), (0, 0)))
    for axes in stages:
        parts = flat.reshape(lax.axis_size(axes), -1, BLOCK)
        flat = jnp.sum(lax.all_to_all(parts, axes, split_axis=0, concat_axis=0, tiled=True), axis=0)
    for axes in reversed(stages):
        spread = jnp.broadcast_to(flat[None], (lax.axis_size(axes), *flat.shape))
        flat = lax.all_to_all(spread, axes, split_axis=0, concat_axis=0, tiled=True).reshape(-1, BLOCK)
    return flat


def hold(values, after):
    return list(lax.optimization_barrier((values, after))[0])


def chunk_count(per):
    return max(k for k in range(1, 6) if per % k == 0)


def phase_sizes(xlocal, groups):
    short = xlocal // 4
    if short % HALF or groups * short % BLOCK:
        short = xlocal // 2
    return [xlocal - short, short]


def local(snapshot):
    xlocal, ylocal, zlocal = snapshot.shape
    groups = lax.axis_size("gx")
    per = ylocal // groups
    chunks = chunk_count(per)
    steps = per // chunks
    starts = [chunk * steps for chunk in range(chunks)]
    talls = phase_sizes(xlocal, groups)
    me = lax.axis_index("gx").astype(jnp.int32).reshape(1)

    long = [(0, talls[0], start, steps) for start in starts]
    cut = per - steps if chunks > 1 else per
    short = [(talls[0], talls[1], 0, cut)]
    short += [(talls[0], talls[1], cut, steps)] if chunks > 1 else []
    packed = pack(me, snapshot, groups, long[:1], 54 * 2**20)
    packed += pack(me, snapshot, groups, long[1:] + short, 44 * 2**20)

    moved = []
    for index, parts in enumerate(packed):
        if index >= 2:
            parts = hold(parts, moved[index - 2])
        moved.append(exchange(parts))

    halves = []
    total = None
    for parts in moved[:chunks]:
        total, made = gram_step(me, parts, [[]], total)
        halves.append(made)
    sums = [total_sum(total, [("gy", "gz"), "gx"])]
    total, at = None, 0
    for parts in moved[chunks:]:
        count = parts[0].shape[0] // steps
        total, made = gram_step(me, hold(parts, sums[0]), halves[at : at + count], total)
        for held, pair in zip(halves[at : at + count], made):
            held.append(pair)
        at += count
    sums.append(total_sum(total, [AXES]))

    mine, turned = factor_step(me, sums, groups, talls)
    outs = [exchange(core_step(me, turned, held, groups, zlocal)) for held in halves]
    return (mine, place(me, outs, starts, ylocal))


def solution(mesh):
    in_specs = (P("gx", "gy", "gz"),)
    out_specs = (P("gx", None), P("gx", "gy", "gz"))
    return jax.shard_map(local, mesh=mesh, in_specs=in_specs, out_specs=out_specs, check_vma=False)
```

```python
import functools

import jax
import jax.numpy as jnp
from jax import lax
from jax.experimental import pallas as pl
from jax.experimental.pallas import tpu as pltpu
from jax.sharding import PartitionSpec as P

RANK = 128
ITERS = 2
BLOCK = 128
SUB = 8
HALF = 16
AXES = ("gx", "gy", "gz")
VMEM = pl.BlockSpec(memory_space=pltpu.VMEM)
SMEM = pl.BlockSpec(memory_space=pltpu.SMEM)
ANY = pl.BlockSpec(memory_space=pl.ANY)
HBM = pl.BlockSpec(memory_space=pltpu.HBM)
SMALL, LARGE = 12 * 2**20, 56 * 2**20
PARAMS = pltpu.CompilerParams(vmem_limit_bytes=SMALL)


def product(left, right, contract=((1,), (0,))):
    return lax.dot_general(
        left, right, (contract, ((), ())), precision=lax.Precision.HIGHEST, preferred_element_type=jnp.float32
    )


def split(value):
    high = value.astype(jnp.bfloat16)
    low = (value - high.astype(jnp.float32)).astype(jnp.bfloat16)
    return high, low


def dot(left, right, contract):
    return lax.dot_general(left, right, (contract, ((), ())), preferred_element_type=jnp.float32)


def pack_kernel(groups, per, pieces, me_ref, snapshot_ref, *refs):
    outs, refs = refs[: groups * len(pieces)], refs[groups * len(pieces) :]
    helds, sems = refs[:-1], refs[-1]
    copies = []
    for index, (x0, tall, start, steps) in enumerate(pieces):
        for shift in [*range(1, groups), 0]:
            owner = lax.rem(me_ref[0] + shift, groups)
            first = pl.multiple_of(owner * per + start, SUB)
            source = snapshot_ref.at[pl.ds(x0, tall), pl.ds(first, steps), :]
            copy = pltpu.make_async_copy(source, helds[index].at[shift], sems.at[index * groups + shift])
            copy.start()
            copies.append((index, shift, copy))
    for index, shift, copy in copies:
        copy.wait()
        for step in range(pieces[index][3]):
            outs[index * groups + shift][step] = helds[index][shift, :, step, :]


def pack(me, snapshot, groups, pieces, limit):
    _, ylocal, zlocal = snapshot.shape
    per = ylocal // groups
    if per % SUB or any(steps % SUB for _, _, _, steps in pieces):
        parts = []
        for x0, tall, start, steps in pieces:
            for shift in range(groups):
                first = lax.rem(me[0] + shift, groups) * per + start
                piece = lax.dynamic_slice_in_dim(snapshot[x0 : x0 + tall], first, steps, 1)
                parts.append(jnp.swapaxes(piece, 0, 1))
    else:
        outs, helds = [], []
        for _, tall, _, steps in pieces:
            outs += [jax.ShapeDtypeStruct((steps, tall, zlocal), jnp.float32)] * groups
            helds.append(pltpu.VMEM((groups, tall, steps, zlocal), jnp.float32))
        parts = pl.pallas_call(
            functools.partial(pack_kernel, groups, per, tuple(pieces)),
            out_shape=tuple(outs),
            in_specs=[SMEM, HBM],
            out_specs=(VMEM,) * len(outs),
            scratch_shapes=[*helds, pltpu.SemaphoreType.DMA((len(outs),))],
            compiler_params=pltpu.CompilerParams(vmem_limit_bytes=limit),
            cost_estimate=pl.CostEstimate(
                flops=0, bytes_accessed=8 * sum(groups * tall * steps * zlocal for _, tall, _, steps in pieces), transcendentals=0
            ),
        )(me, snapshot)
    return [list(parts[at : at + groups]) for at in range(0, len(parts), groups)]


def gram_kernel(first, groups, chunks, earlier, me_ref, *refs):
    parts, refs = refs[:groups], refs[groups:]
    held, refs = refs[: 2 * chunks * earlier], refs[2 * chunks * earlier :]
    old_ref, refs = (None, refs) if first else (refs[0], refs[1:])
    out_ref, made = refs[0], refs[1:]
    wide, tall, zlocal = parts[0].shape
    steps = wide // chunks
    last = ((1,), (1,))
    for chunk in range(chunks):
        high_ref, low_ref = made[2 * chunk : 2 * chunk + 2]
        for shift in range(groups):
            owner = lax.rem(me_ref[0] + groups - shift, groups)
            rows = pl.ds(pl.multiple_of(owner * tall, HALF), tall)
            for step in range(steps):
                high, low = split(parts[shift][chunk * steps + step])
                columns = slice(step * zlocal, (step + 1) * zlocal)
                high_ref[rows, columns] = high
                low_ref[rows, columns] = low
        pairs = held[2 * chunk * earlier : 2 * (chunk + 1) * earlier]
        pairs = [*zip(pairs[::2], pairs[1::2]), (high_ref, low_ref)]
        slot = 0
        for row in range(groups * tall // BLOCK):
            mine = slice(row * BLOCK, (row + 1) * BLOCK)
            for other_high, other_low in pairs:
                upto = slice(0, (row + 1) * BLOCK if other_high is high_ref else other_high.shape[0])
                total = dot(high_ref[mine, :], other_high[upto, :], last)
                total += dot(high_ref[mine, :], other_low[upto, :], last)
                total += dot(low_ref[mine, :], other_high[upto, :], last)
                for column in range(upto.stop // BLOCK):
                    at = slice(slot * BLOCK, (slot + 1) * BLOCK)
                    block = total[:, column * BLOCK : (column + 1) * BLOCK]
                    if chunk:
                        block += out_ref[at, :]
                    elif not first:
                        block += old_ref[at, :]
                    out_ref[at, :] = block
                    slot += 1


def gram_step(me, parts, earlier, old, limit):
    groups, chunks = len(parts), len(earlier)
    wide, tall, zlocal = parts[0].shape
    rows = groups * tall
    before = sum(high.shape[0] for high, _ in earlier[0])
    done, count = before // BLOCK, rows // BLOCK
    slots = done * count + count * (count + 1) // 2
    first = old is None
    half = jax.ShapeDtypeStruct((rows, wide // chunks * zlocal), jnp.bfloat16)
    operands = [me, *parts, *(half for held in earlier for pair in held for half in pair)]
    operands += [] if first else [old]
    total, *made = pl.pallas_call(
        functools.partial(gram_kernel, first, groups, chunks, len(earlier[0])),
        out_shape=(jax.ShapeDtypeStruct((slots * BLOCK, BLOCK), jnp.float32),) + (half,) * (2 * chunks),
        in_specs=[SMEM] + [VMEM] * (len(operands) - 1),
        out_specs=(VMEM,) * (1 + 2 * chunks),
        compiler_params=pltpu.CompilerParams(vmem_limit_bytes=limit),
        cost_estimate=pl.CostEstimate(
            flops=6 * slots * BLOCK * BLOCK * wide * zlocal, bytes_accessed=8 * rows * wide * zlocal, transcendentals=0
        ),
    )(*operands)
    return total, list(zip(made[::2], made[1::2]))


def inverse_cholesky(a_ref, b_ref, w_ref):
    order = a_ref.shape[0]
    wide = (SUB, order)
    below = lax.broadcasted_iota(jnp.int32, wide, 0)
    across = lax.broadcasted_iota(jnp.int32, wide, 1)
    for group in range(order // SUB):
        b_ref[group * SUB : (group + 1) * SUB, :] = jnp.where(across == below + group * SUB, 1.0, 0.0)

    def spread_row(value, row):
        return jnp.broadcast_to(value[row : row + 1, :], wide)

    for panel in range(order // SUB):
        at = slice(panel * SUB, (panel + 1) * SUB)
        a, b = a_ref[at, :], b_ref[at, :]
        columns = [jnp.broadcast_to(a[:, panel * SUB + k : panel * SUB + k + 1], wide) for k in range(SUB)]
        inverses, factors, scale = [], {}, jnp.zeros(wide, jnp.float32)
        for j in range(SUB):
            pivot = spread_row(columns[j], j)
            inverse = 1.0 / pivot
            inverses.append(inverse)
            scale = jnp.where(below == j, lax.rsqrt(pivot), scale)
            lower = jnp.where(below > j, columns[j], 0.0)
            for k in range(j + 1, SUB):
                factors[j, k] = spread_row(columns[k], j) * inverse
                columns[k] = columns[k] - lower * factors[j, k]
            lower = lower * inverse
            a = a - lower * spread_row(a, j)
            b = b - lower * spread_row(b, j)
        w_ref[at, :] = b * scale
        a_rows = [spread_row(a, j) * inverses[j] for j in range(SUB)]
        b_rows = [spread_row(b, j) * inverses[j] for j in range(SUB)]
        for group in range(panel + 1, order // SUB):
            rows = slice(group * SUB, (group + 1) * SUB)
            a, b = a_ref[rows, :], b_ref[rows, :]
            columns = [jnp.broadcast_to(a[:, panel * SUB + k : panel * SUB + k + 1], wide) for k in range(SUB)]
            for j in range(SUB):
                for k in range(j + 1, SUB):
                    columns[k] = columns[k] - columns[j] * factors[j, k]
                a = a - columns[j] * a_rows[j]
                b = b - columns[j] * b_rows[j]
            a_ref[rows, :] = a
            b_ref[rows, :] = b


def factor_kernel(groups, talls, me_ref, *refs):
    phases = len(talls)
    sums, refs = refs[:phases], refs[phases:]
    mine_ref, turned_ref, gram_ref, m_ref, a_ref, b_ref, w_ref = refs
    bases = [groups * sum(talls[:phase]) for phase in range(phases)]
    xlocal = sum(talls)
    for phase, tall in enumerate(talls):
        slot = 0
        first = bases[phase] // BLOCK
        for row in range(first, first + groups * tall // BLOCK):
            for column in range(row + 1):
                block = sums[phase][slot * BLOCK : (slot + 1) * BLOCK, :]
                slot += 1
                gram_ref[row * BLOCK : (row + 1) * BLOCK, column * BLOCK : (column + 1) * BLOCK] = block
                if row != column:
                    gram_ref[column * BLOCK : (column + 1) * BLOCK, row * BLOCK : (row + 1) * BLOCK] = block.T
    lines = []
    for owner in range(-(-RANK // xlocal)):
        for base, tall in zip(bases, talls):
            lines.append(gram_ref[base + owner * tall : base + (owner + 1) * tall, :])
    m_ref[...] = jnp.concatenate(lines, axis=0)[:RANK, :].T

    def step(index, carry):
        m = m_ref[...]
        a_ref[...] = product(m, m, ((0,), (0,)))
        inverse_cholesky(a_ref, b_ref, w_ref)
        basis = product(m, w_ref[...], ((1,), (1,)))
        m_ref[...] = basis

        @pl.when(index < ITERS)
        def _():
            m_ref[...] = product(gram_ref[...], basis)

        return carry

    lax.fori_loop(0, ITERS + 1, step, 0)
    offset = 0
    for base, tall in zip(bases, talls):
        rows = pl.ds(pl.multiple_of(base + me_ref[0] * tall, SUB), tall)
        mine_ref[offset : offset + tall, :] = m_ref[rows, :]
        offset += tall
    turned_ref[...] = m_ref[...].T


def factor_step(me, sums, groups, talls):
    order, xlocal = groups * sum(talls), sum(talls)
    square = pltpu.VMEM((RANK, RANK), jnp.float32)
    return pl.pallas_call(
        functools.partial(factor_kernel, groups, talls),
        out_shape=(
            jax.ShapeDtypeStruct((xlocal, RANK), jnp.float32),
            jax.ShapeDtypeStruct((RANK, order), jnp.float32),
        ),
        in_specs=[SMEM] + [VMEM] * len(sums),
        out_specs=(VMEM, VMEM),
        scratch_shapes=[
            pltpu.VMEM((order, order), jnp.float32),
            pltpu.VMEM((order, RANK), jnp.float32),
            square,
            square,
            square,
        ],
        compiler_params=PARAMS,
    )(me, *sums)


def core_kernel(groups, keep, steps, zlocal, phases, me_ref, turned_ref, *refs):
    highs, lows, outs = refs[:phases], refs[phases : 2 * phases], refs[2 * phases :]
    lines = []
    for shift in range(groups):
        owner = lax.rem(me_ref[0] + shift, groups)
        lines.append(turned_ref[pl.ds(pl.multiple_of(owner * keep, SUB), keep), :])
    high, low = split(jnp.concatenate(lines, axis=0))
    natural = ((1,), (0,))
    total, base = 0.0, 0
    for high_ref, low_ref in zip(highs, lows):
        rows = slice(base, base + high_ref.shape[0])
        base = rows.stop
        total += dot(high[:, rows], high_ref[...], natural)
        total += dot(high[:, rows], low_ref[...], natural)
        total += dot(low[:, rows], high_ref[...], natural)
    for shift in range(groups):
        for step in range(steps):
            outs[shift][:, step, :] = total[shift * keep : (shift + 1) * keep, step * zlocal : (step + 1) * zlocal]


def core_step(me, turned, halves, groups, zlocal):
    order, width = turned.shape[1], halves[0][0].shape[1]
    steps = width // zlocal
    keep = RANK // groups
    return pl.pallas_call(
        functools.partial(core_kernel, groups, keep, steps, zlocal, len(halves)),
        out_shape=(jax.ShapeDtypeStruct((keep, steps, zlocal), jnp.float32),) * groups,
        in_specs=[SMEM] + [VMEM] * (1 + 2 * len(halves)),
        out_specs=(VMEM,) * groups,
        compiler_params=PARAMS,
        cost_estimate=pl.CostEstimate(flops=6 * RANK * order * width, bytes_accessed=6 * order * width, transcendentals=0),
    )(me, turned, *(high for high, _ in halves), *(low for _, low in halves))


def place_kernel(groups, per, starts, steps, me_ref, *refs):
    parts, out_ref, sem = refs[:-2], refs[-2], refs[-1]
    copies = []
    for chunk, start in enumerate(starts):
        for shift in range(groups):
            owner = lax.rem(me_ref[0] + groups - shift, groups)
            first = pl.multiple_of(owner * per + start, SUB)
            index = chunk * groups + shift
            copy = pltpu.make_async_copy(parts[index], out_ref.at[:, pl.ds(first, steps), :], sem.at[index])
            copy.start()
            copies.append(copy)
    for copy in copies:
        copy.wait()


def place(me, chunks, starts, ylocal):
    groups = len(chunks[0])
    keep, steps, zlocal = chunks[0][0].shape
    per = ylocal // groups
    shape = (keep, ylocal, zlocal)
    if steps % SUB or per % SUB:
        out = jnp.zeros(shape, jnp.float32)
        for start, parts in zip(starts, chunks):
            for shift, part in enumerate(parts):
                first = lax.rem(me[0] + groups - shift, groups) * per + start
                out = lax.dynamic_update_slice_in_dim(out, part, first, 1)
        return out
    parts = [part for parts in chunks for part in parts]
    return pl.pallas_call(
        functools.partial(place_kernel, groups, per, starts, steps),
        out_shape=jax.ShapeDtypeStruct(shape, jnp.float32),
        in_specs=[SMEM] + [ANY] * len(parts),
        out_specs=ANY,
        scratch_shapes=[pltpu.SemaphoreType.DMA((len(parts),))],
        compiler_params=PARAMS,
    )(me, *parts)


def exchange(parts):
    groups = len(parts)
    moved = [parts[0]]
    for shift in range(1, groups):
        moved.append(lax.ppermute(parts[shift], "gx", [(i, (i + shift) % groups) for i in range(groups)]))
    return moved


def total_sum(blocks, stages):
    rows = blocks.shape[0]
    flat = jnp.pad(blocks, ((0, -rows % lax.axis_size(AXES)), (0, 0)))
    for axes in stages:
        parts = flat.reshape(lax.axis_size(axes), -1, BLOCK)
        flat = jnp.sum(lax.all_to_all(parts, axes, split_axis=0, concat_axis=0, tiled=True), axis=0)
    for axes in reversed(stages):
        spread = jnp.broadcast_to(flat[None], (lax.axis_size(axes), *flat.shape))
        flat = lax.all_to_all(spread, axes, split_axis=0, concat_axis=0, tiled=True).reshape(-1, BLOCK)
    return flat


def hold(values, after):
    return list(lax.optimization_barrier((values, after))[0])


def chunk_count(per):
    return max(k for k in range(1, 6) if per % k == 0)


def local(snapshot):
    xlocal, ylocal, zlocal = snapshot.shape
    groups = lax.axis_size("gx")
    per = ylocal // groups
    chunks = chunk_count(per)
    steps = per // chunks
    starts = [chunk * steps for chunk in range(chunks)]
    talls = [xlocal]
    me = lax.axis_index("gx").astype(jnp.int32).reshape(1)

    pieces = [(0, xlocal, start, steps) for start in starts]
    packed = pack(me, snapshot, groups, pieces[:1], 54 * 2**20)
    if chunks > 1:
        packed += pack(me, snapshot, groups, pieces[1:], 44 * 2**20)

    moved = []
    for index, parts in enumerate(packed):
        if index >= 2:
            parts = hold(parts, moved[index - 2])
        moved.append(exchange(parts))

    halves = []
    total = None
    for index, parts in enumerate(moved):
        limit = SMALL if index == chunks - 1 else LARGE
        total, made = gram_step(me, parts, [[]], total, limit)
        halves.append(made)
    sums = [total_sum(total, [AXES])]

    mine, turned = factor_step(me, sums, groups, talls)
    outs = []
    for held in halves[-1:] + halves[:-1]:
        if len(outs) == 1:
            (turned,) = hold([turned], parts[0])
        parts = core_step(me, turned, held, groups, zlocal)
        outs.append(exchange(hold(parts, outs[-2]) if len(outs) >= 2 else parts))
    return (mine, place(me, outs, starts[-1:] + starts[:-1], ylocal))


def solution(mesh):
    in_specs = (P("gx", "gy", "gz"),)
    out_specs = (P("gx", None), P("gx", "gy", "gz"))
    return jax.shard_map(local, mesh=mesh, in_specs=in_specs, out_specs=out_specs, check_vma=False)
```

```python
import functools
import math

import jax
import jax.numpy as jnp
from jax import lax
from jax.experimental import pallas as pl
from jax.experimental.pallas import tpu as pltpu
from jax.sharding import PartitionSpec as P

RANK = 128
ITERS = 2
BLOCK = 128
SUB = 8
HALF = 16
CHIPS = ("gx", "gy", "gu")
CORES = "gc"
VMEM = pl.BlockSpec(memory_space=pltpu.VMEM)
SMEM = pl.BlockSpec(memory_space=pltpu.SMEM)
ANY = pl.BlockSpec(memory_space=pl.ANY)
HBM = pl.BlockSpec(memory_space=pltpu.HBM)
SMALL, LARGE = 12 * 2**20, 56 * 2**20
PARAMS = pltpu.CompilerParams(vmem_limit_bytes=SMALL)


def product(left, right, contract=((1,), (0,))):
    return lax.dot_general(
        left, right, (contract, ((), ())), precision=lax.Precision.HIGHEST, preferred_element_type=jnp.float32
    )


def split(value):
    high = value.astype(jnp.bfloat16)
    low = (value - high.astype(jnp.float32)).astype(jnp.bfloat16)
    return high, low


def dot(left, right, contract):
    return lax.dot_general(left, right, (contract, ((), ())), preferred_element_type=jnp.float32)


def pack_kernel(groups, per, pieces, me_ref, snapshot_ref, *refs):
    outs, refs = refs[: groups * len(pieces)], refs[groups * len(pieces) :]
    helds, sems = refs[:-1], refs[-1]
    copies = []
    for index, (x0, tall, start, steps) in enumerate(pieces):
        for shift in [*range(1, groups), 0]:
            owner = lax.rem(me_ref[0] + shift, groups)
            first = pl.multiple_of(owner * per + start, SUB)
            source = snapshot_ref.at[pl.ds(x0, tall), pl.ds(first, steps), :]
            copy = pltpu.make_async_copy(source, helds[index].at[shift], sems.at[index * groups + shift])
            copy.start()
            copies.append((index, shift, copy))
    for index, shift, copy in copies:
        copy.wait()
        for step in range(pieces[index][3]):
            outs[index * groups + shift][step] = helds[index][shift, :, step, :]


def pack(me, snapshot, groups, pieces, limit):
    _, ylocal, zlocal = snapshot.shape
    per = ylocal // groups
    if per % SUB or any(steps % SUB for _, _, _, steps in pieces):
        parts = []
        for x0, tall, start, steps in pieces:
            for shift in range(groups):
                first = lax.rem(me[0] + shift, groups) * per + start
                piece = lax.dynamic_slice_in_dim(snapshot[x0 : x0 + tall], first, steps, 1)
                parts.append(jnp.swapaxes(piece, 0, 1))
    else:
        outs, helds = [], []
        for _, tall, _, steps in pieces:
            outs += [jax.ShapeDtypeStruct((steps, tall, zlocal), jnp.float32)] * groups
            helds.append(pltpu.VMEM((groups, tall, steps, zlocal), jnp.float32))
        parts = pl.pallas_call(
            functools.partial(pack_kernel, groups, per, tuple(pieces)),
            out_shape=tuple(outs),
            in_specs=[SMEM, HBM],
            out_specs=(VMEM,) * len(outs),
            scratch_shapes=[*helds, pltpu.SemaphoreType.DMA((len(outs),))],
            compiler_params=pltpu.CompilerParams(vmem_limit_bytes=limit),
            cost_estimate=pl.CostEstimate(
                flops=0, bytes_accessed=8 * sum(groups * tall * steps * zlocal for _, tall, _, steps in pieces), transcendentals=0
            ),
        )(me, snapshot)
    return [list(parts[at : at + groups]) for at in range(0, len(parts), groups)]


def gram_kernel(first, groups, chunks, earlier, me_ref, *refs):
    parts, refs = refs[:groups], refs[groups:]
    held, refs = refs[: 2 * chunks * earlier], refs[2 * chunks * earlier :]
    old_ref, refs = (None, refs) if first else (refs[0], refs[1:])
    out_ref, made = refs[0], refs[1:]
    wide, tall, zlocal = parts[0].shape
    steps = wide // chunks
    last = ((1,), (1,))
    for chunk in range(chunks):
        high_ref, low_ref = made[2 * chunk : 2 * chunk + 2]
        for shift in range(groups):
            owner = lax.rem(me_ref[0] + groups - shift, groups)
            rows = pl.ds(pl.multiple_of(owner * tall, HALF), tall)
            for step in range(steps):
                high, low = split(parts[shift][chunk * steps + step])
                columns = slice(step * zlocal, (step + 1) * zlocal)
                high_ref[rows, columns] = high
                low_ref[rows, columns] = low
        pairs = held[2 * chunk * earlier : 2 * (chunk + 1) * earlier]
        pairs = [*zip(pairs[::2], pairs[1::2]), (high_ref, low_ref)]
        slot = 0
        for row in range(groups * tall // BLOCK):
            mine = slice(row * BLOCK, (row + 1) * BLOCK)
            for other_high, other_low in pairs:
                upto = slice(0, (row + 1) * BLOCK if other_high is high_ref else other_high.shape[0])
                total = dot(high_ref[mine, :], other_high[upto, :], last)
                total += dot(high_ref[mine, :], other_low[upto, :], last)
                total += dot(low_ref[mine, :], other_high[upto, :], last)
                for column in range(upto.stop // BLOCK):
                    at = slice(slot * BLOCK, (slot + 1) * BLOCK)
                    block = total[:, column * BLOCK : (column + 1) * BLOCK]
                    if chunk:
                        block += out_ref[at, :]
                    elif not first:
                        block += old_ref[at, :]
                    out_ref[at, :] = block
                    slot += 1


def gram_step(me, parts, earlier, old, limit):
    groups, chunks = len(parts), len(earlier)
    wide, tall, zlocal = parts[0].shape
    rows = groups * tall
    before = sum(high.shape[0] for high, _ in earlier[0])
    done, count = before // BLOCK, rows // BLOCK
    slots = done * count + count * (count + 1) // 2
    first = old is None
    half = jax.ShapeDtypeStruct((rows, wide // chunks * zlocal), jnp.bfloat16)
    operands = [me, *parts, *(half for held in earlier for pair in held for half in pair)]
    operands += [] if first else [old]
    total, *made = pl.pallas_call(
        functools.partial(gram_kernel, first, groups, chunks, len(earlier[0])),
        out_shape=(jax.ShapeDtypeStruct((slots * BLOCK, BLOCK), jnp.float32),) + (half,) * (2 * chunks),
        in_specs=[SMEM] + [VMEM] * (len(operands) - 1),
        out_specs=(VMEM,) * (1 + 2 * chunks),
        compiler_params=pltpu.CompilerParams(vmem_limit_bytes=limit),
        cost_estimate=pl.CostEstimate(
            flops=6 * slots * BLOCK * BLOCK * wide * zlocal, bytes_accessed=8 * rows * wide * zlocal, transcendentals=0
        ),
    )(*operands)
    return total, list(zip(made[::2], made[1::2]))


def inverse_cholesky(a_ref, b_ref, w_ref):
    order = a_ref.shape[0]
    wide = (SUB, order)
    below = lax.broadcasted_iota(jnp.int32, wide, 0)
    across = lax.broadcasted_iota(jnp.int32, wide, 1)
    for group in range(order // SUB):
        b_ref[group * SUB : (group + 1) * SUB, :] = jnp.where(across == below + group * SUB, 1.0, 0.0)

    def spread_row(value, row):
        return jnp.broadcast_to(value[row : row + 1, :], wide)

    for panel in range(order // SUB):
        at = slice(panel * SUB, (panel + 1) * SUB)
        a, b = a_ref[at, :], b_ref[at, :]
        columns = [jnp.broadcast_to(a[:, panel * SUB + k : panel * SUB + k + 1], wide) for k in range(SUB)]
        inverses, factors, scale = [], {}, jnp.zeros(wide, jnp.float32)
        for j in range(0, SUB, 2):
            pivot, beside, corner = spread_row(columns[j], j), spread_row(columns[j + 1], j), spread_row(columns[j + 1], j + 1)
            minor = pivot * corner - beside * beside
            inverse = 1.0 / pivot
            second = pivot * (1.0 / minor)
            inverses += [inverse, second]
            scale = jnp.where(below == j, lax.rsqrt(pivot), scale)
            scale = jnp.where(below == j + 1, lax.rsqrt(minor * inverse), scale)
            factors[j, j + 1] = beside * inverse
            lower = jnp.where(below > j, columns[j], 0.0)
            after = jnp.where(below > j + 1, columns[j + 1] - columns[j] * factors[j, j + 1], 0.0)
            for k in range(j + 2, SUB):
                factors[j, k] = spread_row(columns[k], j) * inverse
                factors[j + 1, k] = (spread_row(columns[k], j + 1) - beside * factors[j, k]) * second
                columns[k] = columns[k] - lower * factors[j, k] - after * factors[j + 1, k]
            lower, after = lower * inverse, after * second
            a = a - lower * spread_row(a, j)
            b = b - lower * spread_row(b, j)
            a = a - after * spread_row(a, j + 1)
            b = b - after * spread_row(b, j + 1)
        w_ref[at, :] = b * scale
        a_rows = [spread_row(a, j) * inverses[j] for j in range(SUB)]
        b_rows = [spread_row(b, j) * inverses[j] for j in range(SUB)]
        for group in range(panel + 1, order // SUB):
            rows = slice(group * SUB, (group + 1) * SUB)
            a, b = a_ref[rows, :], b_ref[rows, :]
            columns = [jnp.broadcast_to(a[:, panel * SUB + k : panel * SUB + k + 1], wide) for k in range(SUB)]
            for j in range(SUB):
                for k in range(j + 1, SUB):
                    columns[k] = columns[k] - columns[j] * factors[j, k]
                a = a - columns[j] * a_rows[j]
                b = b - columns[j] * b_rows[j]
            a_ref[rows, :] = a
            b_ref[rows, :] = b


def factor_kernel(groups, xlocal, me_ref, core_ref, own_ref, other_ref, mine_ref, turned_ref, gram_ref, m_ref, a_ref, b_ref, w_ref):
    first = core_ref[0] == 0
    halves = own_ref.shape[0]
    for row in range(groups * xlocal // BLOCK):
        for column in range(row + 1):
            at = (row * (row + 1) // 2 + column) * BLOCK
            low = at < halves
            at = slice(at % halves, at % halves + BLOCK)
            own, other = own_ref[at, :], other_ref[at, :]
            block = jnp.where(first, own, other) if low else jnp.where(first, other, own)
            gram_ref[row * BLOCK : (row + 1) * BLOCK, column * BLOCK : (column + 1) * BLOCK] = block
            if row != column:
                gram_ref[column * BLOCK : (column + 1) * BLOCK, row * BLOCK : (row + 1) * BLOCK] = block.T
    m_ref[...] = gram_ref[:, :RANK]

    def step(index, carry):
        m = m_ref[...]
        cross = product(m, m, ((0,), (0,)))
        diagonal = lax.broadcasted_iota(jnp.int32, cross.shape, 0) == lax.broadcasted_iota(jnp.int32, cross.shape, 1)
        diagonal = jnp.where(diagonal, cross, 0.0)
        across = lax.rsqrt(jnp.sum(diagonal, axis=0, keepdims=True))
        down = lax.rsqrt(jnp.sum(diagonal, axis=1, keepdims=True))
        a_ref[...] = cross * across * down
        inverse_cholesky(a_ref, b_ref, w_ref)
        basis = product(m, w_ref[...] * across, ((1,), (1,)))
        m_ref[...] = basis

        @pl.when(index < ITERS)
        def _():
            m_ref[...] = product(gram_ref[...], basis)

        return carry

    lax.fori_loop(0, ITERS + 1, step, 0)
    mine_ref[...] = m_ref[pl.ds(pl.multiple_of(me_ref[0] * xlocal, SUB), xlocal), :]
    turned_ref[...] = m_ref[...].T


def factor_step(me, core, own, other, groups, xlocal):
    order = groups * xlocal
    square = pltpu.VMEM((RANK, RANK), jnp.float32)
    return pl.pallas_call(
        functools.partial(factor_kernel, groups, xlocal),
        out_shape=(
            jax.ShapeDtypeStruct((xlocal, RANK), jnp.float32),
            jax.ShapeDtypeStruct((RANK, order), jnp.float32),
        ),
        in_specs=[SMEM, SMEM, VMEM, VMEM],
        out_specs=(VMEM, VMEM),
        scratch_shapes=[
            pltpu.VMEM((order, order), jnp.float32),
            pltpu.VMEM((order, RANK), jnp.float32),
            square,
            square,
            square,
        ],
        compiler_params=PARAMS,
    )(me, core, own, other)


def core_kernel(groups, keep, steps, zlocal, phases, me_ref, turned_ref, *refs):
    highs, lows, outs = refs[:phases], refs[phases : 2 * phases], refs[2 * phases :]
    lines = []
    for shift in range(groups):
        owner = lax.rem(me_ref[0] + shift, groups)
        lines.append(turned_ref[pl.ds(pl.multiple_of(owner * keep, SUB), keep), :])
    high, low = split(jnp.concatenate(lines, axis=0))
    natural = ((1,), (0,))
    total, base = 0.0, 0
    for high_ref, low_ref in zip(highs, lows):
        rows = slice(base, base + high_ref.shape[0])
        base = rows.stop
        total += dot(high[:, rows], high_ref[...], natural)
        total += dot(high[:, rows], low_ref[...], natural)
        total += dot(low[:, rows], high_ref[...], natural)
    for shift in range(groups):
        for step in range(steps):
            outs[shift][:, step, :] = total[shift * keep : (shift + 1) * keep, step * zlocal : (step + 1) * zlocal]


def core_step(me, turned, halves, groups, zlocal):
    order, width = turned.shape[1], halves[0][0].shape[1]
    steps = width // zlocal
    keep = RANK // groups
    return pl.pallas_call(
        functools.partial(core_kernel, groups, keep, steps, zlocal, len(halves)),
        out_shape=(jax.ShapeDtypeStruct((keep, steps, zlocal), jnp.float32),) * groups,
        in_specs=[SMEM] + [VMEM] * (1 + 2 * len(halves)),
        out_specs=(VMEM,) * groups,
        compiler_params=PARAMS,
        cost_estimate=pl.CostEstimate(flops=6 * RANK * order * width, bytes_accessed=6 * order * width, transcendentals=0),
    )(me, turned, *(high for high, _ in halves), *(low for _, low in halves))


def place_kernel(groups, per, starts, steps, me_ref, *refs):
    parts, out_ref, sem = refs[:-2], refs[-2], refs[-1]
    copies = []
    for chunk, start in enumerate(starts):
        for shift in range(groups):
            owner = lax.rem(me_ref[0] + groups - shift, groups)
            first = pl.multiple_of(owner * per + start, SUB)
            index = chunk * groups + shift
            copy = pltpu.make_async_copy(parts[index], out_ref.at[:, pl.ds(first, steps), :], sem.at[index])
            copy.start()
            copies.append(copy)
    for copy in copies:
        copy.wait()


def place(me, chunks, starts, ylocal):
    groups = len(chunks[0])
    keep, steps, zlocal = chunks[0][0].shape
    per = ylocal // groups
    shape = (keep, ylocal, zlocal)
    if steps % SUB or per % SUB:
        out = jnp.zeros(shape, jnp.float32)
        for start, parts in zip(starts, chunks):
            for shift, part in enumerate(parts):
                first = lax.rem(me[0] + groups - shift, groups) * per + start
                out = lax.dynamic_update_slice_in_dim(out, part, first, 1)
        return out
    parts = [part for parts in chunks for part in parts]
    return pl.pallas_call(
        functools.partial(place_kernel, groups, per, starts, steps),
        out_shape=jax.ShapeDtypeStruct(shape, jnp.float32),
        in_specs=[SMEM] + [ANY] * len(parts),
        out_specs=ANY,
        scratch_shapes=[pltpu.SemaphoreType.DMA((len(parts),))],
        compiler_params=PARAMS,
    )(me, *parts)


def exchange(parts):
    groups = len(parts)
    moved = [parts[0]]
    for shift in range(1, groups):
        moved.append(lax.ppermute(parts[shift], "gx", [(i, (i + shift) % groups) for i in range(groups)]))
    return moved


def total_sum(blocks, core):
    chips = lax.axis_size(CHIPS)
    swap = [(0, 1), (1, 0)]
    unit = math.lcm(2 * chips, 2 * BLOCK)
    blocks = jnp.pad(blocks, ((0, -blocks.shape[0] % unit), (0, 0)))
    half = blocks.shape[0] // 2
    other = lax.ppermute(lax.dynamic_slice_in_dim(blocks, (1 - core[0]) * half, half), CORES, swap)
    own = lax.dynamic_slice_in_dim(blocks, core[0] * half, half) + other
    parts = own.reshape(chips, -1, BLOCK)
    share = jnp.sum(lax.all_to_all(parts, CHIPS, split_axis=0, concat_axis=0, tiled=True), axis=0)
    spread = jnp.broadcast_to(share[None], parts.shape)
    own = lax.all_to_all(spread, CHIPS, split_axis=0, concat_axis=0, tiled=True).reshape(half, BLOCK)
    return own, lax.ppermute(own, CORES, swap)


def hold(values, after):
    return list(lax.optimization_barrier((values, after))[0])


def chunk_count(per):
    return max(k for k in range(1, 6) if per % k == 0)


def local(snapshot):
    xlocal, ylocal, zlocal = snapshot.shape
    groups = lax.axis_size("gx")
    per = ylocal // groups
    chunks = chunk_count(per)
    steps = per // chunks
    starts = [chunk * steps for chunk in range(chunks)]
    me = lax.axis_index("gx").astype(jnp.int32).reshape(1)
    core = lax.axis_index(CORES).astype(jnp.int32).reshape(1)

    pieces = [(0, xlocal, start, steps) for start in starts]
    packed = pack(me, snapshot, groups, pieces[:1], 54 * 2**20)
    if chunks > 1:
        packed += pack(me, snapshot, groups, pieces[1:], 44 * 2**20)

    moved = []
    for index, parts in enumerate(packed):
        if index >= 2:
            parts = hold(parts, moved[index - 2])
        moved.append(exchange(parts))

    halves = []
    total = None
    for parts in moved:
        total, made = gram_step(me, parts, [[]], total, SMALL)
        halves.append(made)
    own, other = total_sum(total, core)
    mine, turned = factor_step(me, core, own, other, groups, xlocal)
    outs = []
    for held in halves[-1:] + halves[:-1]:
        if len(outs) == 1:
            (turned,) = hold([turned], parts[0])
        parts = core_step(me, turned, held, groups, zlocal)
        outs.append(exchange(hold(parts, outs[-2]) if len(outs) >= 2 else parts))
    return (mine, place(me, outs, starts[-1:] + starts[:-1], ylocal))


def solution(mesh):
    gx, gy, gz = mesh.devices.shape
    mesh = jax.sharding.Mesh(mesh.devices.reshape(gx, gy, gz // 2, 2), (*CHIPS, CORES))
    grid = P("gx", "gy", ("gu", CORES))
    return jax.shard_map(local, mesh=mesh, in_specs=(grid,), out_specs=(P("gx", None), grid), check_vma=False)
```

```python
import functools
import math

import jax
import jax.numpy as jnp
from jax import lax
from jax.experimental import pallas as pl
from jax.experimental.pallas import tpu as pltpu
from jax.sharding import PartitionSpec as P

RANK = 128
ITERS = 2
BLOCK = 128
SUB = 8
HALF = 16
CHIPS = ("gx", "gy", "gu")
CORES = "gc"
VMEM = pl.BlockSpec(memory_space=pltpu.VMEM)
SMEM = pl.BlockSpec(memory_space=pltpu.SMEM)
ANY = pl.BlockSpec(memory_space=pl.ANY)
HBM = pl.BlockSpec(memory_space=pltpu.HBM)
SMALL, LARGE = 12 * 2**20, 54 * 2**20
PARAMS = pltpu.CompilerParams(vmem_limit_bytes=SMALL)


def product(left, right, contract=((1,), (0,))):
    return lax.dot_general(
        left, right, (contract, ((), ())), precision=lax.Precision.HIGHEST, preferred_element_type=jnp.float32
    )


def split(value):
    high = value.astype(jnp.bfloat16)
    low = (value - high.astype(jnp.float32)).astype(jnp.bfloat16)
    return high, low


def dot(left, right, contract):
    return lax.dot_general(left, right, (contract, ((), ())), preferred_element_type=jnp.float32)


def pack_kernel(groups, per, pieces, me_ref, snapshot_ref, *refs):
    outs, refs = refs[: groups * len(pieces)], refs[groups * len(pieces) :]
    helds, sems = refs[:-1], refs[-1]
    copies = []
    for index, (x0, tall, start, steps) in enumerate(pieces):
        for shift in [*range(1, groups), 0]:
            owner = lax.rem(me_ref[0] + shift, groups)
            first = pl.multiple_of(owner * per + start, SUB)
            source = snapshot_ref.at[pl.ds(x0, tall), pl.ds(first, steps), :]
            copy = pltpu.make_async_copy(source, helds[index].at[shift], sems.at[index * groups + shift])
            copy.start()
            copies.append((index, shift, copy))
    for index, shift, copy in copies:
        copy.wait()
        for step in range(pieces[index][3]):
            outs[index * groups + shift][step] = helds[index][shift, :, step, :]


def pack(me, snapshot, groups, pieces, limit):
    _, ylocal, zlocal = snapshot.shape
    per = ylocal // groups
    if per % SUB or any(steps % SUB for _, _, _, steps in pieces):
        parts = []
        for x0, tall, start, steps in pieces:
            for shift in range(groups):
                first = lax.rem(me[0] + shift, groups) * per + start
                piece = lax.dynamic_slice_in_dim(snapshot[x0 : x0 + tall], first, steps, 1)
                parts.append(jnp.swapaxes(piece, 0, 1))
    else:
        outs, helds = [], []
        for _, tall, _, steps in pieces:
            outs += [jax.ShapeDtypeStruct((steps, tall, zlocal), jnp.float32)] * groups
            helds.append(pltpu.VMEM((groups, tall, steps, zlocal), jnp.float32))
        parts = pl.pallas_call(
            functools.partial(pack_kernel, groups, per, tuple(pieces)),
            out_shape=tuple(outs),
            in_specs=[SMEM, HBM],
            out_specs=(VMEM,) * len(outs),
            scratch_shapes=[*helds, pltpu.SemaphoreType.DMA((len(outs),))],
            compiler_params=pltpu.CompilerParams(vmem_limit_bytes=limit),
            cost_estimate=pl.CostEstimate(
                flops=0, bytes_accessed=8 * sum(groups * tall * steps * zlocal for _, tall, _, steps in pieces), transcendentals=0
            ),
        )(me, snapshot)
    return [list(parts[at : at + groups]) for at in range(0, len(parts), groups)]


def gram_kernel(first, final, groups, me_ref, core_ref, *refs):
    parts, refs = refs[:groups], refs[groups:]
    old_ref, refs = (None, refs) if first else (refs[0], refs[1:])
    out_ref, (high_ref, low_ref) = (refs[-1], refs[2:4]) if final else (refs[0], refs[1:])
    steps, tall, zlocal = parts[0].shape
    last = ((1,), (1,))
    for shift in range(groups):
        owner = lax.rem(me_ref[0] + groups - shift, groups)
        rows = pl.ds(pl.multiple_of(owner * tall, HALF), tall)
        for step in range(steps):
            high, low = split(parts[shift][step])
            columns = slice(step * zlocal, (step + 1) * zlocal)
            high_ref[rows, columns] = high
            low_ref[rows, columns] = low
    slot = 0
    for row in range(groups * tall // BLOCK):
        mine = slice(row * BLOCK, (row + 1) * BLOCK)
        upto = slice(0, (row + 1) * BLOCK)
        total = dot(high_ref[mine, :], high_ref[upto, :], last)
        total += dot(high_ref[mine, :], low_ref[upto, :], last)
        total += dot(low_ref[mine, :], high_ref[upto, :], last)
        for column in range(row + 1):
            at = slice(slot * BLOCK, (slot + 1) * BLOCK)
            block = total[:, column * BLOCK : (column + 1) * BLOCK]
            out_ref[at, :] = block if first else block + old_ref[at, :]
            slot += 1
    if final:
        own_ref, other_ref = refs[:2]
        half = own_ref.shape[0]
        if slot * BLOCK < 2 * half:
            out_ref[slot * BLOCK :, :] = jnp.zeros((2 * half - slot * BLOCK, BLOCK), jnp.float32)
        low, high = out_ref[:half, :], out_ref[half:, :]
        own_ref[...] = jnp.where(core_ref[0] == 0, low, high)
        other_ref[...] = jnp.where(core_ref[0] == 0, high, low)


def gram_step(me, core, parts, old, unit):
    groups = len(parts)
    steps, tall, zlocal = parts[0].shape
    rows = groups * tall
    count = rows // BLOCK
    slots = count * (count + 1) // 2
    first, final = old is None, unit is not None
    half = jax.ShapeDtypeStruct((rows, steps * zlocal), jnp.bfloat16)
    operands = [me, core, *parts] + ([] if first else [old])
    height = slots * BLOCK
    sums = [jax.ShapeDtypeStruct((height, BLOCK), jnp.float32)]
    scratch = []
    if final:
        height += -height % unit
        sums = [jax.ShapeDtypeStruct((height // 2, BLOCK), jnp.float32)] * 2
        scratch = [pltpu.VMEM((height, BLOCK), jnp.float32)]
    *sums, high, low = pl.pallas_call(
        functools.partial(gram_kernel, first, final, groups),
        out_shape=(*sums, half, half),
        in_specs=[SMEM, SMEM] + [VMEM] * (len(operands) - 2),
        out_specs=(VMEM,) * (len(sums) + 2),
        scratch_shapes=scratch,
        compiler_params=PARAMS,
        cost_estimate=pl.CostEstimate(
            flops=6 * slots * BLOCK * BLOCK * steps * zlocal, bytes_accessed=8 * rows * steps * zlocal, transcendentals=0
        ),
    )(*operands)
    return sums, [(high, low)]


def inverse_cholesky(a_ref, b_ref, w_ref):
    order = a_ref.shape[0]
    wide = (SUB, order)
    below = lax.broadcasted_iota(jnp.int32, wide, 0)
    across = lax.broadcasted_iota(jnp.int32, wide, 1)
    for group in range(order // SUB):
        b_ref[group * SUB : (group + 1) * SUB, :] = jnp.where(across == below + group * SUB, 1.0, 0.0)

    def spread_row(value, row):
        return jnp.broadcast_to(value[row : row + 1, :], wide)

    for panel in range(order // SUB):
        at = slice(panel * SUB, (panel + 1) * SUB)
        a, b = a_ref[at, :], b_ref[at, :]
        columns = [jnp.broadcast_to(a[:, panel * SUB + k : panel * SUB + k + 1], wide) for k in range(SUB)]
        inverses, factors, scale = [], {}, jnp.zeros(wide, jnp.float32)
        for j in range(0, SUB, 2):
            pivot, beside, corner = spread_row(columns[j], j), spread_row(columns[j + 1], j), spread_row(columns[j + 1], j + 1)
            minor = pivot * corner - beside * beside
            inverse = 1.0 / pivot
            second = pivot * (1.0 / minor)
            inverses += [inverse, second]
            scale = jnp.where(below == j, lax.rsqrt(pivot), scale)
            scale = jnp.where(below == j + 1, lax.rsqrt(minor * inverse), scale)
            factors[j, j + 1] = beside * inverse
            lower = jnp.where(below > j, columns[j], 0.0)
            after = jnp.where(below > j + 1, columns[j + 1] - columns[j] * factors[j, j + 1], 0.0)
            for k in range(j + 2, SUB):
                factors[j, k] = spread_row(columns[k], j) * inverse
                factors[j + 1, k] = (spread_row(columns[k], j + 1) - beside * factors[j, k]) * second
                columns[k] = columns[k] - lower * factors[j, k] - after * factors[j + 1, k]
            lower, after = lower * inverse, after * second
            a = a - lower * spread_row(a, j)
            b = b - lower * spread_row(b, j)
            a = a - after * spread_row(a, j + 1)
            b = b - after * spread_row(b, j + 1)
        w_ref[at, :] = b * scale
        a_rows = [spread_row(a, j) * inverses[j] for j in range(SUB)]
        b_rows = [spread_row(b, j) * inverses[j] for j in range(SUB)]
        for group in range(panel + 1, order // SUB):
            rows = slice(group * SUB, (group + 1) * SUB)
            a, b = a_ref[rows, :], b_ref[rows, :]
            columns = [jnp.broadcast_to(a[:, panel * SUB + k : panel * SUB + k + 1], wide) for k in range(SUB)]
            for j in range(SUB):
                for k in range(j + 1, SUB):
                    columns[k] = columns[k] - columns[j] * factors[j, k]
                a = a - columns[j] * a_rows[j]
                b = b - columns[j] * b_rows[j]
            a_ref[rows, :] = a
            b_ref[rows, :] = b


def factor_kernel(groups, xlocal, me_ref, core_ref, own_ref, other_ref, mine_ref, turned_ref, gram_ref, m_ref, a_ref, b_ref, w_ref):
    first = core_ref[0] == 0
    halves = own_ref.shape[0]
    for row in range(groups * xlocal // BLOCK):
        for column in range(row + 1):
            at = (row * (row + 1) // 2 + column) * BLOCK
            low = at < halves
            at = slice(at % halves, at % halves + BLOCK)
            own, other = own_ref[at, :], other_ref[at, :]
            block = jnp.where(first, own, other) if low else jnp.where(first, other, own)
            gram_ref[row * BLOCK : (row + 1) * BLOCK, column * BLOCK : (column + 1) * BLOCK] = block
            if row != column:
                gram_ref[column * BLOCK : (column + 1) * BLOCK, row * BLOCK : (row + 1) * BLOCK] = block.T
    m_ref[...] = gram_ref[:, :RANK]

    def step(index, carry):
        m = m_ref[...]
        cross = product(m, m, ((0,), (0,)))
        diagonal = lax.broadcasted_iota(jnp.int32, cross.shape, 0) == lax.broadcasted_iota(jnp.int32, cross.shape, 1)
        diagonal = jnp.where(diagonal, cross, 0.0)
        across = lax.rsqrt(jnp.sum(diagonal, axis=0, keepdims=True))
        down = lax.rsqrt(jnp.sum(diagonal, axis=1, keepdims=True))
        a_ref[...] = cross * across * down
        inverse_cholesky(a_ref, b_ref, w_ref)
        basis = product(m, w_ref[...] * across, ((1,), (1,)))
        m_ref[...] = basis

        @pl.when(index < ITERS)
        def _():
            m_ref[...] = product(gram_ref[...], basis)

        return carry

    lax.fori_loop(0, ITERS + 1, step, 0)
    mine_ref[...] = m_ref[pl.ds(pl.multiple_of(me_ref[0] * xlocal, SUB), xlocal), :]
    turned_ref[...] = m_ref[...].T


def factor_step(me, core, own, other, groups, xlocal):
    order = groups * xlocal
    square = pltpu.VMEM((RANK, RANK), jnp.float32)
    return pl.pallas_call(
        functools.partial(factor_kernel, groups, xlocal),
        out_shape=(
            jax.ShapeDtypeStruct((xlocal, RANK), jnp.float32),
            jax.ShapeDtypeStruct((RANK, order), jnp.float32),
        ),
        in_specs=[SMEM, SMEM, VMEM, VMEM],
        out_specs=(VMEM, VMEM),
        scratch_shapes=[
            pltpu.VMEM((order, order), jnp.float32),
            pltpu.VMEM((order, RANK), jnp.float32),
            square,
            square,
            square,
        ],
        compiler_params=PARAMS,
    )(me, core, own, other)


def core_kernel(groups, keep, steps, zlocal, phases, me_ref, turned_ref, *refs):
    highs, lows, outs = refs[:phases], refs[phases : 2 * phases], refs[2 * phases :]
    lines = []
    for shift in range(groups):
        owner = lax.rem(me_ref[0] + shift, groups)
        lines.append(turned_ref[pl.ds(pl.multiple_of(owner * keep, SUB), keep), :])
    high, low = split(jnp.concatenate(lines, axis=0))
    natural = ((1,), (0,))
    total, base = 0.0, 0
    for high_ref, low_ref in zip(highs, lows):
        rows = slice(base, base + high_ref.shape[0])
        base = rows.stop
        total += dot(high[:, rows], high_ref[...], natural)
        total += dot(high[:, rows], low_ref[...], natural)
        total += dot(low[:, rows], high_ref[...], natural)
    for shift in range(groups):
        for step in range(steps):
            outs[shift][:, step, :] = total[shift * keep : (shift + 1) * keep, step * zlocal : (step + 1) * zlocal]


def core_step(me, turned, halves, groups, zlocal):
    order, width = turned.shape[1], halves[0][0].shape[1]
    steps = width // zlocal
    keep = RANK // groups
    return pl.pallas_call(
        functools.partial(core_kernel, groups, keep, steps, zlocal, len(halves)),
        out_shape=(jax.ShapeDtypeStruct((keep, steps, zlocal), jnp.float32),) * groups,
        in_specs=[SMEM] + [VMEM] * (1 + 2 * len(halves)),
        out_specs=(VMEM,) * groups,
        compiler_params=PARAMS,
        cost_estimate=pl.CostEstimate(flops=6 * RANK * order * width, bytes_accessed=6 * order * width, transcendentals=0),
    )(me, turned, *(high for high, _ in halves), *(low for _, low in halves))


def place_kernel(groups, per, starts, steps, me_ref, *refs):
    parts, out_ref, sem = refs[:-2], refs[-2], refs[-1]
    copies = []
    for chunk, start in enumerate(starts):
        for shift in range(groups):
            owner = lax.rem(me_ref[0] + groups - shift, groups)
            first = pl.multiple_of(owner * per + start, SUB)
            index = chunk * groups + shift
            copy = pltpu.make_async_copy(parts[index], out_ref.at[:, pl.ds(first, steps), :], sem.at[index])
            copy.start()
            copies.append(copy)
    for copy in copies:
        copy.wait()


def place(me, chunks, starts, ylocal):
    groups = len(chunks[0])
    keep, steps, zlocal = chunks[0][0].shape
    per = ylocal // groups
    shape = (keep, ylocal, zlocal)
    if steps % SUB or per % SUB:
        out = jnp.zeros(shape, jnp.float32)
        for start, parts in zip(starts, chunks):
            for shift, part in enumerate(parts):
                first = lax.rem(me[0] + groups - shift, groups) * per + start
                out = lax.dynamic_update_slice_in_dim(out, part, first, 1)
        return out
    parts = [part for parts in chunks for part in parts]
    return pl.pallas_call(
        functools.partial(place_kernel, groups, per, starts, steps),
        out_shape=jax.ShapeDtypeStruct(shape, jnp.float32),
        in_specs=[SMEM] + [ANY] * len(parts),
        out_specs=ANY,
        scratch_shapes=[pltpu.SemaphoreType.DMA((len(parts),))],
        compiler_params=PARAMS,
    )(me, *parts)


def exchange(parts):
    groups = len(parts)
    moved = [parts[0]]
    for shift in range(1, groups):
        moved.append(lax.ppermute(parts[shift], "gx", [(i, (i + shift) % groups) for i in range(groups)]))
    return moved


def total_sum(own, other):
    swap = [(0, 1), (1, 0)]
    own = own + lax.ppermute(other, CORES, swap)
    parts = own.reshape(lax.axis_size(CHIPS), -1, BLOCK)
    share = jnp.sum(lax.all_to_all(parts, CHIPS, split_axis=0, concat_axis=0, tiled=True), axis=0)
    spread = jnp.broadcast_to(share[None], parts.shape)
    own = lax.all_to_all(spread, CHIPS, split_axis=0, concat_axis=0, tiled=True).reshape(own.shape)
    return own, lax.ppermute(own, CORES, swap)


def hold(values, after):
    return list(lax.optimization_barrier((values, after))[0])


def chunk_count(per):
    return max(k for k in range(1, 6) if per % k == 0)


def local(snapshot):
    xlocal, ylocal, zlocal = snapshot.shape
    groups = lax.axis_size("gx")
    per = ylocal // groups
    chunks = chunk_count(per)
    steps = per // chunks
    starts = [chunk * steps for chunk in range(chunks)]
    me = lax.axis_index("gx").astype(jnp.int32).reshape(1)
    core = lax.axis_index(CORES).astype(jnp.int32).reshape(1)

    pieces = [(0, xlocal, start, steps) for start in starts]
    packed = pack(me, snapshot, groups, pieces[:1], LARGE)
    if chunks > 1:
        packed += pack(me, snapshot, groups, pieces[1:], 16 * 2**20)

    moved = []
    for index, parts in enumerate(packed):
        if index >= 2:
            parts = hold(parts, moved[index - 2])
        moved.append(exchange(parts))

    unit = math.lcm(2 * lax.axis_size(CHIPS), 2 * BLOCK)
    halves = []
    sums = [None]
    for index, parts in enumerate(moved):
        sums, made = gram_step(me, core, parts, sums[0], unit if index == chunks - 1 else None)
        halves.append(made)
    own, other = total_sum(*sums)
    mine, turned = factor_step(me, core, own, other, groups, xlocal)
    outs = []
    for held in halves[-1:] + halves[:-1]:
        if len(outs) == 1:
            (turned,) = hold([turned], parts[0])
        parts = core_step(me, turned, held, groups, zlocal)
        outs.append(exchange(hold(parts, outs[-2]) if len(outs) >= 2 else parts))
    return (mine, place(me, outs, starts[-1:] + starts[:-1], ylocal))


def solution(mesh):
    gx, gy, gz = mesh.devices.shape
    mesh = jax.sharding.Mesh(mesh.devices.reshape(gx, gy, gz // 2, 2), (*CHIPS, CORES))
    grid = P("gx", "gy", ("gu", CORES))
    return jax.shard_map(local, mesh=mesh, in_specs=(grid,), out_specs=(P("gx", None), grid), check_vma=False)
```

```python
import functools
import math

import jax
import jax.numpy as jnp
from jax import lax
from jax.experimental import pallas as pl
from jax.experimental.pallas import tpu as pltpu
from jax.sharding import PartitionSpec as P

RANK = 128
ITERS = 2
BLOCK = 128
SUB = 8
HALF = 16
CHIPS = ("gx", "gy", "gu")
CORES = "gc"
VMEM = pl.BlockSpec(memory_space=pltpu.VMEM)
SMEM = pl.BlockSpec(memory_space=pltpu.SMEM)
ANY = pl.BlockSpec(memory_space=pl.ANY)
HBM = pl.BlockSpec(memory_space=pltpu.HBM)
SMALL, LARGE = 12 * 2**20, 54 * 2**20
PARAMS = pltpu.CompilerParams(vmem_limit_bytes=SMALL)


def product(left, right, contract=((1,), (0,))):
    return lax.dot_general(
        left, right, (contract, ((), ())), precision=lax.Precision.HIGHEST, preferred_element_type=jnp.float32
    )


def split(value):
    high = value.astype(jnp.bfloat16)
    low = (value - high.astype(jnp.float32)).astype(jnp.bfloat16)
    return high, low


def dot(left, right, contract):
    return lax.dot_general(left, right, (contract, ((), ())), preferred_element_type=jnp.float32)


def pack_kernel(groups, per, pieces, me_ref, snapshot_ref, *refs):
    outs, refs = refs[: groups * len(pieces)], refs[groups * len(pieces) :]
    helds, sems = refs[:-1], refs[-1]
    copies = []
    for index, (x0, tall, start, steps) in enumerate(pieces):
        for shift in [*range(1, groups), 0]:
            owner = lax.rem(me_ref[0] + shift, groups)
            first = pl.multiple_of(owner * per + start, SUB)
            source = snapshot_ref.at[pl.ds(x0, tall), pl.ds(first, steps), :]
            copy = pltpu.make_async_copy(source, helds[index].at[shift], sems.at[index * groups + shift])
            copy.start()
            copies.append((index, shift, copy))
    for index, shift, copy in copies:
        copy.wait()
        for step in range(pieces[index][3]):
            outs[index * groups + shift][step] = helds[index][shift, :, step, :]


def pack(me, snapshot, groups, pieces, limit):
    _, ylocal, zlocal = snapshot.shape
    per = ylocal // groups
    if per % SUB or any(steps % SUB for _, _, _, steps in pieces):
        parts = []
        for x0, tall, start, steps in pieces:
            for shift in range(groups):
                first = lax.rem(me[0] + shift, groups) * per + start
                piece = lax.dynamic_slice_in_dim(snapshot[x0 : x0 + tall], first, steps, 1)
                parts.append(jnp.swapaxes(piece, 0, 1))
    else:
        outs, helds = [], []
        for _, tall, _, steps in pieces:
            outs += [jax.ShapeDtypeStruct((steps, tall, zlocal), jnp.float32)] * groups
            helds.append(pltpu.VMEM((groups, tall, steps, zlocal), jnp.float32))
        parts = pl.pallas_call(
            functools.partial(pack_kernel, groups, per, tuple(pieces)),
            out_shape=tuple(outs),
            in_specs=[SMEM, HBM],
            out_specs=(VMEM,) * len(outs),
            scratch_shapes=[*helds, pltpu.SemaphoreType.DMA((len(outs),))],
            compiler_params=pltpu.CompilerParams(vmem_limit_bytes=limit),
            cost_estimate=pl.CostEstimate(
                flops=0, bytes_accessed=8 * sum(groups * tall * steps * zlocal for _, tall, _, steps in pieces), transcendentals=0
            ),
        )(me, snapshot)
    return [list(parts[at : at + groups]) for at in range(0, len(parts), groups)]


def gram_kernel(first, final, groups, me_ref, core_ref, *refs):
    parts, refs = refs[:groups], refs[groups:]
    old_ref, refs = (None, refs) if first else (refs[0], refs[1:])
    out_ref, (high_ref, low_ref) = (refs[-1], refs[2:4]) if final else (refs[0], refs[1:])
    steps, tall, zlocal = parts[0].shape
    last = ((1,), (1,))
    for shift in range(groups):
        owner = lax.rem(me_ref[0] + groups - shift, groups)
        rows = pl.ds(pl.multiple_of(owner * tall, HALF), tall)
        for step in range(steps):
            high, low = split(parts[shift][step])
            columns = slice(step * zlocal, (step + 1) * zlocal)
            high_ref[rows, columns] = high
            low_ref[rows, columns] = low
    order = groups * tall
    height = order // BLOCK * (order // BLOCK + 1) // 2 * BLOCK
    big = 2 * BLOCK if order % (2 * BLOCK) == 0 else BLOCK
    ratio = big // BLOCK
    for row in range(order // big):
        left = slice(row * big, (row + 1) * big)
        for column in range(row + 1):
            right = slice(column * big, (column + 1) * big)
            total = dot(high_ref[left, :], high_ref[right, :], last)
            total += dot(high_ref[left, :], low_ref[right, :], last)
            total += dot(low_ref[left, :], high_ref[right, :], last)
            for i in range(ratio):
                for j in range(ratio):
                    r, c = row * ratio + i, column * ratio + j
                    if r < c:
                        continue
                    at = (r * (r + 1) // 2 + c) * BLOCK
                    at = slice(at, at + BLOCK)
                    block = total[i * BLOCK : (i + 1) * BLOCK, j * BLOCK : (j + 1) * BLOCK]
                    out_ref[at, :] = block if first else block + old_ref[at, :]
    if final:
        own_ref, other_ref = refs[:2]
        half = own_ref.shape[0]
        if height < 2 * half:
            out_ref[height:, :] = jnp.zeros((2 * half - height, BLOCK), jnp.float32)
        low, high = out_ref[:half, :], out_ref[half:, :]
        own_ref[...] = jnp.where(core_ref[0] == 0, low, high)
        other_ref[...] = jnp.where(core_ref[0] == 0, high, low)


def gram_step(me, core, parts, old, unit):
    groups = len(parts)
    steps, tall, zlocal = parts[0].shape
    rows = groups * tall
    count = rows // BLOCK
    slots = count * (count + 1) // 2
    first, final = old is None, unit is not None
    half = jax.ShapeDtypeStruct((rows, steps * zlocal), jnp.bfloat16)
    operands = [me, core, *parts] + ([] if first else [old])
    height = slots * BLOCK
    sums = [jax.ShapeDtypeStruct((height, BLOCK), jnp.float32)]
    scratch = []
    if final:
        height += -height % unit
        sums = [jax.ShapeDtypeStruct((height // 2, BLOCK), jnp.float32)] * 2
        scratch = [pltpu.VMEM((height, BLOCK), jnp.float32)]
    *sums, high, low = pl.pallas_call(
        functools.partial(gram_kernel, first, final, groups),
        out_shape=(*sums, half, half),
        in_specs=[SMEM, SMEM] + [VMEM] * (len(operands) - 2),
        out_specs=(VMEM,) * (len(sums) + 2),
        scratch_shapes=scratch,
        compiler_params=PARAMS,
        cost_estimate=pl.CostEstimate(
            flops=6 * slots * BLOCK * BLOCK * steps * zlocal, bytes_accessed=8 * rows * steps * zlocal, transcendentals=0
        ),
    )(*operands)
    return sums, [(high, low)]


def inverse_cholesky(a_ref, b_ref, w_ref):
    order = a_ref.shape[0]
    wide = (SUB, order)
    below = lax.broadcasted_iota(jnp.int32, wide, 0)
    across = lax.broadcasted_iota(jnp.int32, wide, 1)
    for group in range(order // SUB):
        b_ref[group * SUB : (group + 1) * SUB, :] = jnp.where(across == below + group * SUB, 1.0, 0.0)

    def spread_row(value, row):
        return jnp.broadcast_to(value[row : row + 1, :], wide)

    for panel in range(order // SUB):
        at = slice(panel * SUB, (panel + 1) * SUB)
        a, b = a_ref[at, :], b_ref[at, :]
        columns = [jnp.broadcast_to(a[:, panel * SUB + k : panel * SUB + k + 1], wide) for k in range(SUB)]
        inverses, factors, scale = [], {}, jnp.zeros(wide, jnp.float32)
        for j in range(0, SUB, 2):
            pivot, beside, corner = spread_row(columns[j], j), spread_row(columns[j + 1], j), spread_row(columns[j + 1], j + 1)
            minor = pivot * corner - beside * beside
            inverse = 1.0 / pivot
            second = pivot * (1.0 / minor)
            inverses += [inverse, second]
            scale = jnp.where(below == j, lax.rsqrt(pivot), scale)
            scale = jnp.where(below == j + 1, lax.rsqrt(minor * inverse), scale)
            factors[j, j + 1] = beside * inverse
            lower = jnp.where(below > j, columns[j], 0.0)
            after = jnp.where(below > j + 1, columns[j + 1] - columns[j] * factors[j, j + 1], 0.0)
            for k in range(j + 2, SUB):
                factors[j, k] = spread_row(columns[k], j) * inverse
                factors[j + 1, k] = (spread_row(columns[k], j + 1) - beside * factors[j, k]) * second
                columns[k] = columns[k] - lower * factors[j, k] - after * factors[j + 1, k]
            lower, after = lower * inverse, after * second
            a = a - lower * spread_row(a, j)
            b = b - lower * spread_row(b, j)
            a = a - after * spread_row(a, j + 1)
            b = b - after * spread_row(b, j + 1)
        w_ref[at, :] = b * scale
        a_rows = [spread_row(a, j) * inverses[j] for j in range(SUB)]
        b_rows = [spread_row(b, j) * inverses[j] for j in range(SUB)]
        for group in range(panel + 1, order // SUB):
            rows = slice(group * SUB, (group + 1) * SUB)
            a, b = a_ref[rows, :], b_ref[rows, :]
            columns = [jnp.broadcast_to(a[:, panel * SUB + k : panel * SUB + k + 1], wide) for k in range(SUB)]
            for j in range(SUB):
                for k in range(j + 1, SUB):
                    columns[k] = columns[k] - columns[j] * factors[j, k]
                a = a - columns[j] * a_rows[j]
                b = b - columns[j] * b_rows[j]
            a_ref[rows, :] = a
            b_ref[rows, :] = b


def factor_kernel(groups, xlocal, me_ref, core_ref, own_ref, other_ref, mine_ref, turned_ref, gram_ref, m_ref, a_ref, b_ref, w_ref):
    first = core_ref[0] == 0
    halves = own_ref.shape[0]
    for row in range(groups * xlocal // BLOCK):
        for column in range(row + 1):
            at = (row * (row + 1) // 2 + column) * BLOCK
            low = at < halves
            at = slice(at % halves, at % halves + BLOCK)
            own, other = own_ref[at, :], other_ref[at, :]
            block = jnp.where(first, own, other) if low else jnp.where(first, other, own)
            gram_ref[row * BLOCK : (row + 1) * BLOCK, column * BLOCK : (column + 1) * BLOCK] = block
            if row != column:
                gram_ref[column * BLOCK : (column + 1) * BLOCK, row * BLOCK : (row + 1) * BLOCK] = block.T
    m_ref[...] = gram_ref[:, :RANK]

    def step(index, carry):
        m = m_ref[...]
        cross = product(m, m, ((0,), (0,)))
        diagonal = lax.broadcasted_iota(jnp.int32, cross.shape, 0) == lax.broadcasted_iota(jnp.int32, cross.shape, 1)
        diagonal = jnp.where(diagonal, cross, 0.0)
        across = lax.rsqrt(jnp.sum(diagonal, axis=0, keepdims=True))
        down = lax.rsqrt(jnp.sum(diagonal, axis=1, keepdims=True))
        a_ref[...] = cross * across * down
        inverse_cholesky(a_ref, b_ref, w_ref)
        basis = product(m, w_ref[...] * across, ((1,), (1,)))
        m_ref[...] = basis

        @pl.when(index < ITERS)
        def _():
            m_ref[...] = product(gram_ref[...], basis)

        return carry

    lax.fori_loop(0, ITERS + 1, step, 0)
    mine_ref[...] = m_ref[pl.ds(pl.multiple_of(me_ref[0] * xlocal, SUB), xlocal), :]
    turned_ref[...] = m_ref[...].T


def factor_step(me, core, own, other, groups, xlocal):
    order = groups * xlocal
    square = pltpu.VMEM((RANK, RANK), jnp.float32)
    return pl.pallas_call(
        functools.partial(factor_kernel, groups, xlocal),
        out_shape=(
            jax.ShapeDtypeStruct((xlocal, RANK), jnp.float32),
            jax.ShapeDtypeStruct((RANK, order), jnp.float32),
        ),
        in_specs=[SMEM, SMEM, VMEM, VMEM],
        out_specs=(VMEM, VMEM),
        scratch_shapes=[
            pltpu.VMEM((order, order), jnp.float32),
            pltpu.VMEM((order, RANK), jnp.float32),
            square,
            square,
            square,
        ],
        compiler_params=PARAMS,
    )(me, core, own, other)


def core_kernel(groups, keep, steps, zlocal, phases, me_ref, turned_ref, *refs):
    highs, lows, outs = refs[:phases], refs[phases : 2 * phases], refs[2 * phases :]
    lines = []
    for shift in range(groups):
        owner = lax.rem(me_ref[0] + shift, groups)
        lines.append(turned_ref[pl.ds(pl.multiple_of(owner * keep, SUB), keep), :])
    high, low = split(jnp.concatenate(lines, axis=0))
    natural = ((1,), (0,))
    total, base = 0.0, 0
    for high_ref, low_ref in zip(highs, lows):
        rows = slice(base, base + high_ref.shape[0])
        base = rows.stop
        total += dot(high[:, rows], high_ref[...], natural)
        total += dot(high[:, rows], low_ref[...], natural)
        total += dot(low[:, rows], high_ref[...], natural)
    for shift in range(groups):
        for step in range(steps):
            outs[shift][:, step, :] = total[shift * keep : (shift + 1) * keep, step * zlocal : (step + 1) * zlocal]


def core_step(me, turned, halves, groups, zlocal):
    order, width = turned.shape[1], halves[0][0].shape[1]
    steps = width // zlocal
    keep = RANK // groups
    return pl.pallas_call(
        functools.partial(core_kernel, groups, keep, steps, zlocal, len(halves)),
        out_shape=(jax.ShapeDtypeStruct((keep, steps, zlocal), jnp.float32),) * groups,
        in_specs=[SMEM] + [VMEM] * (1 + 2 * len(halves)),
        out_specs=(VMEM,) * groups,
        compiler_params=PARAMS,
        cost_estimate=pl.CostEstimate(flops=6 * RANK * order * width, bytes_accessed=6 * order * width, transcendentals=0),
    )(me, turned, *(high for high, _ in halves), *(low for _, low in halves))


def place_kernel(groups, per, starts, steps, me_ref, *refs):
    parts, out_ref, sem = refs[:-2], refs[-2], refs[-1]
    copies = []
    for chunk, start in enumerate(starts):
        for shift in range(groups):
            owner = lax.rem(me_ref[0] + groups - shift, groups)
            first = pl.multiple_of(owner * per + start, SUB)
            index = chunk * groups + shift
            copy = pltpu.make_async_copy(parts[index], out_ref.at[:, pl.ds(first, steps), :], sem.at[index])
            copy.start()
            copies.append(copy)
    for copy in copies:
        copy.wait()


def place(me, chunks, starts, ylocal):
    groups = len(chunks[0])
    keep, steps, zlocal = chunks[0][0].shape
    per = ylocal // groups
    shape = (keep, ylocal, zlocal)
    if steps % SUB or per % SUB:
        out = jnp.zeros(shape, jnp.float32)
        for start, parts in zip(starts, chunks):
            for shift, part in enumerate(parts):
                first = lax.rem(me[0] + groups - shift, groups) * per + start
                out = lax.dynamic_update_slice_in_dim(out, part, first, 1)
        return out
    parts = [part for parts in chunks for part in parts]
    return pl.pallas_call(
        functools.partial(place_kernel, groups, per, starts, steps),
        out_shape=jax.ShapeDtypeStruct(shape, jnp.float32),
        in_specs=[SMEM] + [ANY] * len(parts),
        out_specs=ANY,
        scratch_shapes=[pltpu.SemaphoreType.DMA((len(parts),))],
        compiler_params=PARAMS,
    )(me, *parts)


def exchange(parts):
    groups = len(parts)
    moved = [parts[0]]
    for shift in range(1, groups):
        moved.append(lax.ppermute(parts[shift], "gx", [(i, (i + shift) % groups) for i in range(groups)]))
    return moved


def add_kernel(left_ref, right_ref, out_ref):
    out_ref[...] = left_ref[...] + right_ref[...]


def spread_kernel(parts_ref, out_ref):
    total = parts_ref[0]
    for index in range(1, parts_ref.shape[0]):
        total += parts_ref[index]
    for index in range(parts_ref.shape[0]):
        out_ref[index] = total


def small_call(kernel, *operands):
    shape = jax.ShapeDtypeStruct(operands[0].shape, jnp.float32)
    specs = [VMEM] * len(operands)
    return pl.pallas_call(kernel, out_shape=shape, in_specs=specs, out_specs=VMEM, compiler_params=PARAMS)(*operands)


def total_sum(own, other):
    swap = [(0, 1), (1, 0)]
    own = small_call(add_kernel, own, lax.ppermute(other, CORES, swap))
    parts = own.reshape(lax.axis_size(CHIPS), -1, BLOCK)
    parts = lax.all_to_all(parts, CHIPS, split_axis=0, concat_axis=0, tiled=True)
    spread = small_call(spread_kernel, parts)
    own = lax.all_to_all(spread, CHIPS, split_axis=0, concat_axis=0, tiled=True).reshape(own.shape)
    return own, lax.ppermute(own, CORES, swap)


def hold(values, after):
    return list(lax.optimization_barrier((values, after))[0])


def chunk_count(per):
    return max(k for k in range(1, 6) if per % k == 0)


def local(snapshot):
    xlocal, ylocal, zlocal = snapshot.shape
    groups = lax.axis_size("gx")
    per = ylocal // groups
    chunks = chunk_count(per)
    steps = per // chunks
    starts = [chunk * steps for chunk in range(chunks)]
    me = lax.axis_index("gx").astype(jnp.int32).reshape(1)
    core = lax.axis_index(CORES).astype(jnp.int32).reshape(1)

    pieces = [(0, xlocal, start, steps) for start in starts]
    packed = pack(me, snapshot, groups, pieces[:1], LARGE)
    if chunks > 1:
        packed += pack(me, snapshot, groups, pieces[1:], 16 * 2**20)

    moved = []
    for index, parts in enumerate(packed):
        if index >= 2:
            parts = hold(parts, moved[index - 2])
        moved.append(exchange(parts))

    unit = math.lcm(2 * lax.axis_size(CHIPS), 2 * BLOCK)
    halves = []
    sums = [None]
    for index, parts in enumerate(moved):
        sums, made = gram_step(me, core, parts, sums[0], unit if index == chunks - 1 else None)
        halves.append(made)
    own, other = total_sum(*sums)
    mine, turned = factor_step(me, core, own, other, groups, xlocal)
    outs = []
    for held in halves[-1:] + halves[:-1]:
        if len(outs) == 1:
            (turned,) = hold([turned], parts[0])
        parts = core_step(me, turned, held, groups, zlocal)
        outs.append(exchange(hold(parts, outs[-2]) if len(outs) >= 2 else parts))
    return (mine, place(me, outs, starts[-1:] + starts[:-1], ylocal))


def solution(mesh):
    gx, gy, gz = mesh.devices.shape
    mesh = jax.sharding.Mesh(mesh.devices.reshape(gx, gy, gz // 2, 2), (*CHIPS, CORES))
    grid = P("gx", "gy", ("gu", CORES))
    return jax.shard_map(local, mesh=mesh, in_specs=(grid,), out_specs=(P("gx", None), grid), check_vma=False)
```

```python
import functools
import math

import jax
import jax.numpy as jnp
from jax import lax
from jax.experimental import pallas as pl
from jax.experimental.pallas import tpu as pltpu
from jax.sharding import PartitionSpec as P

RANK = 128
ITERS = 2
BLOCK = 128
SUB = 8
HALF = 16
CHIPS = ("gx", "gy", "gu")
CORES = "gc"
VMEM = pl.BlockSpec(memory_space=pltpu.VMEM)
SMEM = pl.BlockSpec(memory_space=pltpu.SMEM)
ANY = pl.BlockSpec(memory_space=pl.ANY)
HBM = pl.BlockSpec(memory_space=pltpu.HBM)
SMALL, LARGE = 12 * 2**20, 54 * 2**20
PARAMS = pltpu.CompilerParams(vmem_limit_bytes=SMALL)


def product(left, right, contract=((1,), (0,))):
    return lax.dot_general(
        left, right, (contract, ((), ())), precision=lax.Precision.HIGHEST, preferred_element_type=jnp.float32
    )


def split(value):
    high = value.astype(jnp.bfloat16)
    low = (value - high.astype(jnp.float32)).astype(jnp.bfloat16)
    return high, low


def dot(left, right, contract):
    return lax.dot_general(left, right, (contract, ((), ())), preferred_element_type=jnp.float32)


def pack_kernel(groups, per, pieces, me_ref, snapshot_ref, *refs):
    outs, refs = refs[: groups * len(pieces)], refs[groups * len(pieces) :]
    helds, sems = refs[:-1], refs[-1]
    copies = []
    for index, (x0, tall, start, steps) in enumerate(pieces):
        for shift in [*range(1, groups), 0]:
            owner = lax.rem(me_ref[0] + shift, groups)
            first = pl.multiple_of(owner * per + start, SUB)
            source = snapshot_ref.at[pl.ds(x0, tall), pl.ds(first, steps), :]
            copy = pltpu.make_async_copy(source, helds[index].at[shift], sems.at[index * groups + shift])
            copy.start()
            copies.append((index, shift, copy))
    for index, shift, copy in copies:
        copy.wait()
        for step in range(pieces[index][3]):
            outs[index * groups + shift][step] = helds[index][shift, :, step, :]


def pack(me, snapshot, groups, pieces, limit):
    _, ylocal, zlocal = snapshot.shape
    per = ylocal // groups
    if per % SUB or any(steps % SUB for _, _, _, steps in pieces):
        parts = []
        for x0, tall, start, steps in pieces:
            for shift in range(groups):
                first = lax.rem(me[0] + shift, groups) * per + start
                piece = lax.dynamic_slice_in_dim(snapshot[x0 : x0 + tall], first, steps, 1)
                parts.append(jnp.swapaxes(piece, 0, 1))
    else:
        outs, helds = [], []
        for _, tall, _, steps in pieces:
            outs += [jax.ShapeDtypeStruct((steps, tall, zlocal), jnp.float32)] * groups
            helds.append(pltpu.VMEM((groups, tall, steps, zlocal), jnp.float32))
        parts = pl.pallas_call(
            functools.partial(pack_kernel, groups, per, tuple(pieces)),
            out_shape=tuple(outs),
            in_specs=[SMEM, HBM],
            out_specs=(VMEM,) * len(outs),
            scratch_shapes=[*helds, pltpu.SemaphoreType.DMA((len(outs),))],
            compiler_params=pltpu.CompilerParams(vmem_limit_bytes=limit),
            cost_estimate=pl.CostEstimate(
                flops=0, bytes_accessed=8 * sum(groups * tall * steps * zlocal for _, tall, _, steps in pieces), transcendentals=0
            ),
        )(me, snapshot)
    return [list(parts[at : at + groups]) for at in range(0, len(parts), groups)]


def gram_kernel(first, final, groups, me_ref, core_ref, *refs):
    parts, refs = refs[:groups], refs[groups:]
    old_ref, refs = (None, refs) if first else (refs[0], refs[1:])
    out_ref, (high_ref, low_ref) = (refs[-1], refs[2:4]) if final else (refs[0], refs[1:])
    steps, tall, zlocal = parts[0].shape
    last = ((1,), (1,))
    for shift in range(groups):
        owner = lax.rem(me_ref[0] + groups - shift, groups)
        rows = pl.ds(pl.multiple_of(owner * tall, HALF), tall)
        for step in range(steps):
            high, low = split(parts[shift][step])
            columns = slice(step * zlocal, (step + 1) * zlocal)
            high_ref[rows, columns] = high
            low_ref[rows, columns] = low
    order = groups * tall
    height = order // BLOCK * (order // BLOCK + 1) // 2 * BLOCK
    big = 2 * BLOCK if order % (2 * BLOCK) == 0 else BLOCK
    ratio = big // BLOCK
    for row in range(order // big):
        left = slice(row * big, (row + 1) * big)
        for column in range(row + 1):
            right = slice(column * big, (column + 1) * big)
            total = dot(high_ref[left, :], high_ref[right, :], last)
            total += dot(high_ref[left, :], low_ref[right, :], last)
            total += dot(low_ref[left, :], high_ref[right, :], last)
            for i in range(ratio):
                for j in range(ratio):
                    r, c = row * ratio + i, column * ratio + j
                    if r < c:
                        continue
                    at = (r * (r + 1) // 2 + c) * BLOCK
                    at = slice(at, at + BLOCK)
                    block = total[i * BLOCK : (i + 1) * BLOCK, j * BLOCK : (j + 1) * BLOCK]
                    out_ref[at, :] = block if first else block + old_ref[at, :]
    if final:
        own_ref, other_ref = refs[:2]
        half = own_ref.shape[0]
        if height < 2 * half:
            out_ref[height:, :] = jnp.zeros((2 * half - height, BLOCK), jnp.float32)
        low, high = out_ref[:half, :], out_ref[half:, :]
        own_ref[...] = jnp.where(core_ref[0] == 0, low, high)
        other_ref[...] = jnp.where(core_ref[0] == 0, high, low)


def gram_step(me, core, parts, old, unit):
    groups = len(parts)
    steps, tall, zlocal = parts[0].shape
    rows = groups * tall
    count = rows // BLOCK
    slots = count * (count + 1) // 2
    first, final = old is None, unit is not None
    half = jax.ShapeDtypeStruct((rows, steps * zlocal), jnp.bfloat16)
    operands = [me, core, *parts] + ([] if first else [old])
    height = slots * BLOCK
    sums = [jax.ShapeDtypeStruct((height, BLOCK), jnp.float32)]
    scratch = []
    if final:
        height += -height % unit
        sums = [jax.ShapeDtypeStruct((height // 2, BLOCK), jnp.float32)] * 2
        scratch = [pltpu.VMEM((height, BLOCK), jnp.float32)]
    *sums, high, low = pl.pallas_call(
        functools.partial(gram_kernel, first, final, groups),
        out_shape=(*sums, half, half),
        in_specs=[SMEM, SMEM] + [VMEM] * (len(operands) - 2),
        out_specs=(VMEM,) * (len(sums) + 2),
        scratch_shapes=scratch,
        compiler_params=PARAMS,
        cost_estimate=pl.CostEstimate(
            flops=6 * slots * BLOCK * BLOCK * steps * zlocal, bytes_accessed=8 * rows * steps * zlocal, transcendentals=0
        ),
    )(*operands)
    return sums, [(high, low)]


def inverse_cholesky(a_ref, b_ref, w_ref):
    order = a_ref.shape[0]
    wide = (SUB, order)
    below = lax.broadcasted_iota(jnp.int32, wide, 0)
    across = lax.broadcasted_iota(jnp.int32, wide, 1)
    for group in range(order // SUB):
        b_ref[group * SUB : (group + 1) * SUB, :] = jnp.where(across == below + group * SUB, 1.0, 0.0)

    def spread_row(value, row):
        return jnp.broadcast_to(value[row : row + 1, :], wide)

    for panel in range(order // SUB):
        at = slice(panel * SUB, (panel + 1) * SUB)
        a, b = a_ref[at, :], b_ref[at, :]
        columns = [jnp.broadcast_to(a[:, panel * SUB + k : panel * SUB + k + 1], wide) for k in range(SUB)]
        inverses, factors, scale = [], {}, jnp.zeros(wide, jnp.float32)
        for j in range(0, SUB, 2):
            pivot, beside, corner = spread_row(columns[j], j), spread_row(columns[j + 1], j), spread_row(columns[j + 1], j + 1)
            minor = pivot * corner - beside * beside
            inverse = 1.0 / pivot
            second = pivot * (1.0 / minor)
            inverses += [inverse, second]
            scale = jnp.where(below == j, lax.rsqrt(pivot), scale)
            scale = jnp.where(below == j + 1, lax.rsqrt(minor * inverse), scale)
            factors[j, j + 1] = beside * inverse
            lower = jnp.where(below > j, columns[j], 0.0)
            after = jnp.where(below > j + 1, columns[j + 1] - columns[j] * factors[j, j + 1], 0.0)
            for k in range(j + 2, SUB):
                factors[j, k] = spread_row(columns[k], j) * inverse
                factors[j + 1, k] = (spread_row(columns[k], j + 1) - beside * factors[j, k]) * second
                columns[k] = columns[k] - lower * factors[j, k] - after * factors[j + 1, k]
            lower, after = lower * inverse, after * second
            a = a - lower * spread_row(a, j)
            b = b - lower * spread_row(b, j)
            a = a - after * spread_row(a, j + 1)
            b = b - after * spread_row(b, j + 1)
        w_ref[at, :] = b * scale
        a_rows = [spread_row(a, j) * inverses[j] for j in range(SUB)]
        b_rows = [spread_row(b, j) * inverses[j] for j in range(SUB)]
        for group in range(panel + 1, order // SUB):
            rows = slice(group * SUB, (group + 1) * SUB)
            a, b = a_ref[rows, :], b_ref[rows, :]
            columns = [jnp.broadcast_to(a[:, panel * SUB + k : panel * SUB + k + 1], wide) for k in range(SUB)]
            for j in range(SUB):
                for k in range(j + 1, SUB):
                    columns[k] = columns[k] - columns[j] * factors[j, k]
                a = a - columns[j] * a_rows[j]
                b = b - columns[j] * b_rows[j]
            a_ref[rows, :] = a
            b_ref[rows, :] = b


def factor_kernel(groups, xlocal, me_ref, core_ref, own_ref, other_ref, mine_ref, turned_ref, gram_ref, m_ref, a_ref, b_ref, w_ref):
    first = core_ref[0] == 0
    halves = own_ref.shape[0]
    for row in range(groups * xlocal // BLOCK):
        for column in range(row + 1):
            at = (row * (row + 1) // 2 + column) * BLOCK
            low = at < halves
            at = slice(at % halves, at % halves + BLOCK)
            own, other = own_ref[at, :], other_ref[at, :]
            block = jnp.where(first, own, other) if low else jnp.where(first, other, own)
            gram_ref[row * BLOCK : (row + 1) * BLOCK, column * BLOCK : (column + 1) * BLOCK] = block
            if row != column:
                gram_ref[column * BLOCK : (column + 1) * BLOCK, row * BLOCK : (row + 1) * BLOCK] = block.T
    m_ref[...] = gram_ref[:, :RANK]

    def step(index, carry):
        m = m_ref[...]
        cross = product(m, m, ((0,), (0,)))
        diagonal = lax.broadcasted_iota(jnp.int32, cross.shape, 0) == lax.broadcasted_iota(jnp.int32, cross.shape, 1)
        diagonal = jnp.where(diagonal, cross, 0.0)
        across = lax.rsqrt(jnp.sum(diagonal, axis=0, keepdims=True))
        down = lax.rsqrt(jnp.sum(diagonal, axis=1, keepdims=True))
        a_ref[...] = cross * across * down
        inverse_cholesky(a_ref, b_ref, w_ref)
        basis = product(m, w_ref[...] * across, ((1,), (1,)))
        m_ref[...] = basis

        @pl.when(index < ITERS)
        def _():
            m_ref[...] = product(gram_ref[...], basis)

        return carry

    lax.fori_loop(0, ITERS + 1, step, 0)
    mine_ref[...] = m_ref[pl.ds(pl.multiple_of(me_ref[0] * xlocal, SUB), xlocal), :]
    turned_ref[...] = m_ref[...].T


def factor_step(me, core, own, other, groups, xlocal):
    order = groups * xlocal
    square = pltpu.VMEM((RANK, RANK), jnp.float32)
    return pl.pallas_call(
        functools.partial(factor_kernel, groups, xlocal),
        out_shape=(
            jax.ShapeDtypeStruct((xlocal, RANK), jnp.float32),
            jax.ShapeDtypeStruct((RANK, order), jnp.float32),
        ),
        in_specs=[SMEM, SMEM, VMEM, VMEM],
        out_specs=(VMEM, VMEM),
        scratch_shapes=[
            pltpu.VMEM((order, order), jnp.float32),
            pltpu.VMEM((order, RANK), jnp.float32),
            square,
            square,
            square,
        ],
        compiler_params=PARAMS,
    )(me, core, own, other)


def core_kernel(groups, keep, steps, zlocal, phases, me_ref, turned_ref, *refs):
    highs, lows, outs = refs[:phases], refs[phases : 2 * phases], refs[2 * phases :]
    lines = []
    for shift in range(groups):
        owner = lax.rem(me_ref[0] + shift, groups)
        lines.append(turned_ref[pl.ds(pl.multiple_of(owner * keep, SUB), keep), :])
    high, low = split(jnp.concatenate(lines, axis=0))
    natural = ((1,), (0,))
    total, base = 0.0, 0
    for high_ref, low_ref in zip(highs, lows):
        rows = slice(base, base + high_ref.shape[0])
        base = rows.stop
        total += dot(high[:, rows], high_ref[...], natural)
        total += dot(high[:, rows], low_ref[...], natural)
        total += dot(low[:, rows], high_ref[...], natural)
    for shift in range(groups):
        for step in range(steps):
            outs[shift][:, step, :] = total[shift * keep : (shift + 1) * keep, step * zlocal : (step + 1) * zlocal]


def core_step(me, turned, halves, groups, zlocal):
    order, width = turned.shape[1], halves[0][0].shape[1]
    steps = width // zlocal
    keep = RANK // groups
    return pl.pallas_call(
        functools.partial(core_kernel, groups, keep, steps, zlocal, len(halves)),
        out_shape=(jax.ShapeDtypeStruct((keep, steps, zlocal), jnp.float32),) * groups,
        in_specs=[SMEM] + [VMEM] * (1 + 2 * len(halves)),
        out_specs=(VMEM,) * groups,
        compiler_params=PARAMS,
        cost_estimate=pl.CostEstimate(flops=6 * RANK * order * width, bytes_accessed=6 * order * width, transcendentals=0),
    )(me, turned, *(high for high, _ in halves), *(low for _, low in halves))


def place_kernel(groups, per, starts, steps, me_ref, *refs):
    parts, out_ref, sem = refs[:-2], refs[-2], refs[-1]
    copies = []
    for chunk, start in enumerate(starts):
        for shift in range(groups):
            owner = lax.rem(me_ref[0] + groups - shift, groups)
            first = pl.multiple_of(owner * per + start, SUB)
            index = chunk * groups + shift
            copy = pltpu.make_async_copy(parts[index], out_ref.at[:, pl.ds(first, steps), :], sem.at[index])
            copy.start()
            copies.append(copy)
    for copy in copies:
        copy.wait()


def place(me, chunks, starts, ylocal):
    groups = len(chunks[0])
    keep, steps, zlocal = chunks[0][0].shape
    per = ylocal // groups
    shape = (keep, ylocal, zlocal)
    if steps % SUB or per % SUB:
        out = jnp.zeros(shape, jnp.float32)
        for start, parts in zip(starts, chunks):
            for shift, part in enumerate(parts):
                first = lax.rem(me[0] + groups - shift, groups) * per + start
                out = lax.dynamic_update_slice_in_dim(out, part, first, 1)
        return out
    parts = [part for parts in chunks for part in parts]
    return pl.pallas_call(
        functools.partial(place_kernel, groups, per, starts, steps),
        out_shape=jax.ShapeDtypeStruct(shape, jnp.float32),
        in_specs=[SMEM] + [ANY] * len(parts),
        out_specs=ANY,
        scratch_shapes=[pltpu.SemaphoreType.DMA((len(parts),))],
        compiler_params=PARAMS,
    )(me, *parts)


def exchange(parts):
    groups = len(parts)
    moved = [parts[0]]
    for shift in range(1, groups):
        moved.append(lax.ppermute(parts[shift], "gx", [(i, (i + shift) % groups) for i in range(groups)]))
    return moved


def add_kernel(left_ref, right_ref, out_ref):
    out_ref[...] = left_ref[...] + right_ref[...]


def spread_kernel(parts_ref, out_ref):
    total = parts_ref[0]
    for index in range(1, parts_ref.shape[0]):
        total += parts_ref[index]
    for index in range(parts_ref.shape[0]):
        out_ref[index] = total


def small_call(kernel, *operands):
    shape = jax.ShapeDtypeStruct(operands[0].shape, jnp.float32)
    specs = [VMEM] * len(operands)
    return pl.pallas_call(kernel, out_shape=shape, in_specs=specs, out_specs=VMEM, compiler_params=PARAMS)(*operands)


def total_sum(own, other):
    swap = [(0, 1), (1, 0)]
    own = small_call(add_kernel, own, lax.ppermute(other, CORES, swap))
    parts = own.reshape(lax.axis_size(CHIPS), -1, BLOCK)
    parts = lax.all_to_all(parts, CHIPS, split_axis=0, concat_axis=0, tiled=True)
    spread = small_call(spread_kernel, parts)
    own = lax.all_to_all(spread, CHIPS, split_axis=0, concat_axis=0, tiled=True).reshape(own.shape)
    return own, lax.ppermute(own, CORES, swap)


def hold(values, after):
    return list(lax.optimization_barrier((values, after))[0])


def chunk_count(per):
    return max(k for k in range(1, 6) if per % k == 0)


def local(snapshot):
    xlocal, ylocal, zlocal = snapshot.shape
    groups = lax.axis_size("gx")
    per = ylocal // groups
    chunks = chunk_count(per)
    steps = per // chunks
    starts = [chunk * steps for chunk in range(chunks)]
    me = lax.axis_index("gx").astype(jnp.int32).reshape(1)
    core = lax.axis_index(CORES).astype(jnp.int32).reshape(1)

    pieces = [(0, xlocal, start, steps) for start in starts]
    packed = pack(me, snapshot, groups, pieces[:1], LARGE)
    if chunks > 1:
        packed += [parts for piece in pieces[1:] for parts in pack(me, snapshot, groups, [piece], SMALL)]

    moved = []
    for index, parts in enumerate(packed):
        if index >= 2:
            parts = hold(parts, moved[index - 2])
        moved.append(exchange(parts))

    unit = math.lcm(2 * lax.axis_size(CHIPS), 2 * BLOCK)
    halves = []
    sums = [None]
    for index, parts in enumerate(moved):
        sums, made = gram_step(me, core, parts, sums[0], unit if index == chunks - 1 else None)
        halves.append(made)
    own, other = total_sum(*sums)
    mine, turned = factor_step(me, core, own, other, groups, xlocal)
    outs = []
    for held in halves[-1:] + halves[:-1]:
        if len(outs) == 1:
            (turned,) = hold([turned], parts[0])
        parts = core_step(me, turned, held, groups, zlocal)
        outs.append(exchange(hold(parts, outs[-2]) if len(outs) >= 2 else parts))
    return (mine, place(me, outs, starts[-1:] + starts[:-1], ylocal))


def solution(mesh):
    gx, gy, gz = mesh.devices.shape
    mesh = jax.sharding.Mesh(mesh.devices.reshape(gx, gy, gz // 2, 2), (*CHIPS, CORES))
    grid = P("gx", "gy", ("gu", CORES))
    return jax.shard_map(local, mesh=mesh, in_specs=(grid,), out_specs=(P("gx", None), grid), check_vma=False)
```

```python
import functools
import math

import jax
import jax.numpy as jnp
from jax import lax
from jax.experimental import pallas as pl
from jax.experimental.pallas import tpu as pltpu
from jax.sharding import PartitionSpec as P

RANK = 128
ITERS = 2
BLOCK = 128
SUB = 8
HALF = 16
CHIPS = ("gx", "gy", "gu")
CORES = "gc"
VMEM = pl.BlockSpec(memory_space=pltpu.VMEM)
SMEM = pl.BlockSpec(memory_space=pltpu.SMEM)
ANY = pl.BlockSpec(memory_space=pl.ANY)
HBM = pl.BlockSpec(memory_space=pltpu.HBM)
SMALL, LARGE = 12 * 2**20, 54 * 2**20
PARAMS = pltpu.CompilerParams(vmem_limit_bytes=SMALL)


def product(left, right, contract=((1,), (0,))):
    return lax.dot_general(
        left, right, (contract, ((), ())), precision=lax.Precision.HIGHEST, preferred_element_type=jnp.float32
    )


def split(value):
    high = value.astype(jnp.bfloat16)
    low = (value - high.astype(jnp.float32)).astype(jnp.bfloat16)
    return high, low


def dot(left, right, contract):
    return lax.dot_general(left, right, (contract, ((), ())), preferred_element_type=jnp.float32)


def pack_kernel(groups, per, pieces, me_ref, snapshot_ref, *refs):
    outs, refs = refs[: groups * len(pieces)], refs[groups * len(pieces) :]
    helds, sems = refs[:-1], refs[-1]
    copies = []
    for index, (x0, tall, start, steps) in enumerate(pieces):
        for shift in [*range(1, groups), 0]:
            owner = lax.rem(me_ref[0] + shift, groups)
            first = pl.multiple_of(owner * per + start, SUB)
            source = snapshot_ref.at[pl.ds(x0, tall), pl.ds(first, steps), :]
            copy = pltpu.make_async_copy(source, helds[index].at[shift], sems.at[index * groups + shift])
            copy.start()
            copies.append((index, shift, copy))
    for index, shift, copy in copies:
        copy.wait()
        for step in range(pieces[index][3]):
            outs[index * groups + shift][step] = helds[index][shift, :, step, :]


def pack(me, snapshot, groups, pieces, limit):
    _, ylocal, zlocal = snapshot.shape
    per = ylocal // groups
    if per % SUB or any(steps % SUB for _, _, _, steps in pieces):
        parts = []
        for x0, tall, start, steps in pieces:
            for shift in range(groups):
                first = lax.rem(me[0] + shift, groups) * per + start
                piece = lax.dynamic_slice_in_dim(snapshot[x0 : x0 + tall], first, steps, 1)
                parts.append(jnp.swapaxes(piece, 0, 1))
    else:
        outs, helds = [], []
        for _, tall, _, steps in pieces:
            outs += [jax.ShapeDtypeStruct((steps, tall, zlocal), jnp.float32)] * groups
            helds.append(pltpu.VMEM((groups, tall, steps, zlocal), jnp.float32))
        parts = pl.pallas_call(
            functools.partial(pack_kernel, groups, per, tuple(pieces)),
            out_shape=tuple(outs),
            in_specs=[SMEM, HBM],
            out_specs=(VMEM,) * len(outs),
            scratch_shapes=[*helds, pltpu.SemaphoreType.DMA((len(outs),))],
            compiler_params=pltpu.CompilerParams(vmem_limit_bytes=limit),
            cost_estimate=pl.CostEstimate(
                flops=0, bytes_accessed=8 * sum(groups * tall * steps * zlocal for _, tall, _, steps in pieces), transcendentals=0
            ),
        )(me, snapshot)
    return [list(parts[at : at + groups]) for at in range(0, len(parts), groups)]


def gram_kernel(first, final, groups, me_ref, core_ref, *refs):
    parts, refs = refs[:groups], refs[groups:]
    old_ref, refs = (None, refs) if first else (refs[0], refs[1:])
    out_ref, (high_ref, low_ref) = (refs[-1], refs[2:4]) if final else (refs[0], refs[1:])
    steps, tall, zlocal = parts[0].shape
    last = ((1,), (1,))
    for shift in range(groups):
        owner = lax.rem(me_ref[0] + groups - shift, groups)
        rows = pl.ds(pl.multiple_of(owner * tall, HALF), tall)
        for step in range(steps):
            high, low = split(parts[shift][step])
            columns = slice(step * zlocal, (step + 1) * zlocal)
            high_ref[rows, columns] = high
            low_ref[rows, columns] = low
    order = groups * tall
    height = order // BLOCK * (order // BLOCK + 1) // 2 * BLOCK
    big = 2 * BLOCK if order % (2 * BLOCK) == 0 else BLOCK
    ratio = big // BLOCK
    for row in range(order // big):
        left = slice(row * big, (row + 1) * big)
        for column in range(row + 1):
            right = slice(column * big, (column + 1) * big)
            total = dot(high_ref[left, :], high_ref[right, :], last)
            total += dot(high_ref[left, :], low_ref[right, :], last)
            total += dot(low_ref[left, :], high_ref[right, :], last)
            for i in range(ratio):
                for j in range(ratio):
                    r, c = row * ratio + i, column * ratio + j
                    if r < c:
                        continue
                    at = (r * (r + 1) // 2 + c) * BLOCK
                    at = slice(at, at + BLOCK)
                    block = total[i * BLOCK : (i + 1) * BLOCK, j * BLOCK : (j + 1) * BLOCK]
                    out_ref[at, :] = block if first else block + old_ref[at, :]
    if final:
        own_ref, other_ref = refs[:2]
        half = own_ref.shape[0]
        if height < 2 * half:
            out_ref[height:, :] = jnp.zeros((2 * half - height, BLOCK), jnp.float32)
        low, high = out_ref[:half, :], out_ref[half:, :]
        own_ref[...] = jnp.where(core_ref[0] == 0, low, high)
        other_ref[...] = jnp.where(core_ref[0] == 0, high, low)


def gram_step(me, core, parts, old, unit):
    groups = len(parts)
    steps, tall, zlocal = parts[0].shape
    rows = groups * tall
    count = rows // BLOCK
    slots = count * (count + 1) // 2
    first, final = old is None, unit is not None
    half = jax.ShapeDtypeStruct((rows, steps * zlocal), jnp.bfloat16)
    operands = [me, core, *parts] + ([] if first else [old])
    height = slots * BLOCK
    sums = [jax.ShapeDtypeStruct((height, BLOCK), jnp.float32)]
    scratch = []
    if final:
        height += -height % unit
        sums = [jax.ShapeDtypeStruct((height // 2, BLOCK), jnp.float32)] * 2
        scratch = [pltpu.VMEM((height, BLOCK), jnp.float32)]
    *sums, high, low = pl.pallas_call(
        functools.partial(gram_kernel, first, final, groups),
        out_shape=(*sums, half, half),
        in_specs=[SMEM, SMEM] + [VMEM] * (len(operands) - 2),
        out_specs=(VMEM,) * (len(sums) + 2),
        scratch_shapes=scratch,
        compiler_params=PARAMS,
        cost_estimate=pl.CostEstimate(
            flops=6 * slots * BLOCK * BLOCK * steps * zlocal, bytes_accessed=8 * rows * steps * zlocal, transcendentals=0
        ),
    )(*operands)
    return sums, [(high, low)]


def inverse_cholesky(a_ref, b_ref, w_ref):
    order = a_ref.shape[0]
    wide = (SUB, order)
    below = lax.broadcasted_iota(jnp.int32, wide, 0)
    across = lax.broadcasted_iota(jnp.int32, wide, 1)
    for group in range(order // SUB):
        b_ref[group * SUB : (group + 1) * SUB, :] = jnp.where(across == below + group * SUB, 1.0, 0.0)

    def spread_row(value, row):
        return jnp.broadcast_to(value[row : row + 1, :], wide)

    for panel in range(order // SUB):
        at = slice(panel * SUB, (panel + 1) * SUB)
        a, b = a_ref[at, :], b_ref[at, :]
        columns = [jnp.broadcast_to(a[:, panel * SUB + k : panel * SUB + k + 1], wide) for k in range(SUB)]
        inverses, factors, scale = [], {}, jnp.zeros(wide, jnp.float32)
        for j in range(0, SUB, 2):
            pivot, beside, corner = spread_row(columns[j], j), spread_row(columns[j + 1], j), spread_row(columns[j + 1], j + 1)
            minor = pivot * corner - beside * beside
            inverse = 1.0 / pivot
            second = pivot * (1.0 / minor)
            inverses += [inverse, second]
            scale = jnp.where(below == j, lax.rsqrt(pivot), scale)
            scale = jnp.where(below == j + 1, lax.rsqrt(minor * inverse), scale)
            factors[j, j + 1] = beside * inverse
            lower = jnp.where(below > j, columns[j], 0.0)
            after = jnp.where(below > j + 1, columns[j + 1] - columns[j] * factors[j, j + 1], 0.0)
            for k in range(j + 2, SUB):
                factors[j, k] = spread_row(columns[k], j) * inverse
                factors[j + 1, k] = (spread_row(columns[k], j + 1) - beside * factors[j, k]) * second
                columns[k] = columns[k] - lower * factors[j, k] - after * factors[j + 1, k]
            lower, after = lower * inverse, after * second
            a = a - lower * spread_row(a, j)
            b = b - lower * spread_row(b, j)
            a = a - after * spread_row(a, j + 1)
            b = b - after * spread_row(b, j + 1)
        w_ref[at, :] = b * scale
        a_rows = [spread_row(a, j) * inverses[j] for j in range(SUB)]
        b_rows = [spread_row(b, j) * inverses[j] for j in range(SUB)]
        for group in range(panel + 1, order // SUB):
            rows = slice(group * SUB, (group + 1) * SUB)
            a, b = a_ref[rows, :], b_ref[rows, :]
            columns = [jnp.broadcast_to(a[:, panel * SUB + k : panel * SUB + k + 1], wide) for k in range(SUB)]
            for j in range(SUB):
                for k in range(j + 1, SUB):
                    columns[k] = columns[k] - columns[j] * factors[j, k]
                a = a - columns[j] * a_rows[j]
                b = b - columns[j] * b_rows[j]
            a_ref[rows, :] = a
            b_ref[rows, :] = b


def factor_kernel(groups, xlocal, me_ref, core_ref, own_ref, other_ref, mine_ref, turned_ref, gram_ref, m_ref, a_ref, b_ref, w_ref):
    first = core_ref[0] == 0
    halves = own_ref.shape[0]
    for row in range(groups * xlocal // BLOCK):
        for column in range(row + 1):
            at = (row * (row + 1) // 2 + column) * BLOCK
            low = at < halves
            at = slice(at % halves, at % halves + BLOCK)
            own, other = own_ref[at, :], other_ref[at, :]
            block = jnp.where(first, own, other) if low else jnp.where(first, other, own)
            gram_ref[row * BLOCK : (row + 1) * BLOCK, column * BLOCK : (column + 1) * BLOCK] = block
            if row != column:
                gram_ref[column * BLOCK : (column + 1) * BLOCK, row * BLOCK : (row + 1) * BLOCK] = block.T
    m_ref[...] = gram_ref[:, :RANK]

    def step(index, carry):
        m = m_ref[...]
        cross = product(m, m, ((0,), (0,)))
        diagonal = lax.broadcasted_iota(jnp.int32, cross.shape, 0) == lax.broadcasted_iota(jnp.int32, cross.shape, 1)
        diagonal = jnp.where(diagonal, cross, 0.0)
        across = lax.rsqrt(jnp.sum(diagonal, axis=0, keepdims=True))
        down = lax.rsqrt(jnp.sum(diagonal, axis=1, keepdims=True))
        a_ref[...] = cross * across * down
        inverse_cholesky(a_ref, b_ref, w_ref)
        basis = product(m, w_ref[...] * across, ((1,), (1,)))
        m_ref[...] = basis

        @pl.when(index < ITERS)
        def _():
            m_ref[...] = product(gram_ref[...], basis)

        return carry

    lax.fori_loop(0, ITERS + 1, step, 0)
    mine_ref[...] = m_ref[pl.ds(pl.multiple_of(me_ref[0] * xlocal, SUB), xlocal), :]
    turned_ref[...] = m_ref[...].T


def factor_step(me, core, own, other, groups, xlocal):
    order = groups * xlocal
    square = pltpu.VMEM((RANK, RANK), jnp.float32)
    return pl.pallas_call(
        functools.partial(factor_kernel, groups, xlocal),
        out_shape=(
            jax.ShapeDtypeStruct((xlocal, RANK), jnp.float32),
            jax.ShapeDtypeStruct((RANK, order), jnp.float32),
        ),
        in_specs=[SMEM, SMEM, VMEM, VMEM],
        out_specs=(VMEM, VMEM),
        scratch_shapes=[
            pltpu.VMEM((order, order), jnp.float32),
            pltpu.VMEM((order, RANK), jnp.float32),
            square,
            square,
            square,
        ],
        compiler_params=PARAMS,
    )(me, core, own, other)


def core_kernel(groups, keep, steps, zlocal, phases, me_ref, turned_ref, *refs):
    highs, lows, outs = refs[:phases], refs[phases : 2 * phases], refs[2 * phases :]
    lines = []
    for shift in range(groups):
        owner = lax.rem(me_ref[0] + shift, groups)
        lines.append(turned_ref[pl.ds(pl.multiple_of(owner * keep, SUB), keep), :])
    high, low = split(jnp.concatenate(lines, axis=0))
    natural = ((1,), (0,))
    total, base = 0.0, 0
    for high_ref, low_ref in zip(highs, lows):
        rows = slice(base, base + high_ref.shape[0])
        base = rows.stop
        total += dot(high[:, rows], high_ref[...], natural)
        total += dot(high[:, rows], low_ref[...], natural)
        total += dot(low[:, rows], high_ref[...], natural)
    for shift in range(groups):
        for step in range(steps):
            outs[shift][:, step, :] = total[shift * keep : (shift + 1) * keep, step * zlocal : (step + 1) * zlocal]


def core_step(me, turned, halves, groups, zlocal):
    order, width = turned.shape[1], halves[0][0].shape[1]
    steps = width // zlocal
    keep = RANK // groups
    return pl.pallas_call(
        functools.partial(core_kernel, groups, keep, steps, zlocal, len(halves)),
        out_shape=(jax.ShapeDtypeStruct((keep, steps, zlocal), jnp.float32),) * groups,
        in_specs=[SMEM] + [VMEM] * (1 + 2 * len(halves)),
        out_specs=(VMEM,) * groups,
        compiler_params=PARAMS,
        cost_estimate=pl.CostEstimate(flops=6 * RANK * order * width, bytes_accessed=6 * order * width, transcendentals=0),
    )(me, turned, *(high for high, _ in halves), *(low for _, low in halves))


def place_kernel(groups, per, starts, steps, me_ref, *refs):
    parts, out_ref, sem = refs[:-2], refs[-2], refs[-1]
    copies = []
    for chunk, start in enumerate(starts):
        for shift in range(groups):
            owner = lax.rem(me_ref[0] + groups - shift, groups)
            first = pl.multiple_of(owner * per + start, SUB)
            index = chunk * groups + shift
            copy = pltpu.make_async_copy(parts[index], out_ref.at[:, pl.ds(first, steps), :], sem.at[index])
            copy.start()
            copies.append(copy)
    for copy in copies:
        copy.wait()


def place(me, chunks, starts, ylocal):
    groups = len(chunks[0])
    keep, steps, zlocal = chunks[0][0].shape
    per = ylocal // groups
    shape = (keep, ylocal, zlocal)
    if steps % SUB or per % SUB:
        out = jnp.zeros(shape, jnp.float32)
        for start, parts in zip(starts, chunks):
            for shift, part in enumerate(parts):
                first = lax.rem(me[0] + groups - shift, groups) * per + start
                out = lax.dynamic_update_slice_in_dim(out, part, first, 1)
        return out
    parts = [part for parts in chunks for part in parts]
    return pl.pallas_call(
        functools.partial(place_kernel, groups, per, starts, steps),
        out_shape=jax.ShapeDtypeStruct(shape, jnp.float32),
        in_specs=[SMEM] + [ANY] * len(parts),
        out_specs=ANY,
        scratch_shapes=[pltpu.SemaphoreType.DMA((len(parts),))],
        compiler_params=PARAMS,
    )(me, *parts)


def exchange(parts):
    groups = len(parts)
    moved = [parts[0]]
    for shift in range(1, groups):
        moved.append(lax.ppermute(parts[shift], "gx", [(i, (i + shift) % groups) for i in range(groups)]))
    return moved


def add_kernel(left_ref, right_ref, out_ref):
    out_ref[...] = left_ref[...] + right_ref[...]


def spread_kernel(parts_ref, out_ref):
    total = parts_ref[0]
    for index in range(1, parts_ref.shape[0]):
        total += parts_ref[index]
    for index in range(parts_ref.shape[0]):
        out_ref[index] = total


def small_call(kernel, *operands):
    shape = jax.ShapeDtypeStruct(operands[0].shape, jnp.float32)
    specs = [VMEM] * len(operands)
    return pl.pallas_call(kernel, out_shape=shape, in_specs=specs, out_specs=VMEM, compiler_params=PARAMS)(*operands)


def total_sum(own, other):
    swap = [(0, 1), (1, 0)]
    own = small_call(add_kernel, own, lax.ppermute(other, CORES, swap))
    parts = own.reshape(lax.axis_size(CHIPS), -1, BLOCK)
    parts = lax.all_to_all(parts, CHIPS, split_axis=0, concat_axis=0, tiled=True)
    spread = small_call(spread_kernel, parts)
    own = lax.all_to_all(spread, CHIPS, split_axis=0, concat_axis=0, tiled=True).reshape(own.shape)
    return own, lax.ppermute(own, CORES, swap)


def hold(values, after):
    return list(lax.optimization_barrier((values, after))[0])


def chunk_count(per):
    return max(k for k in range(1, 6) if per % k == 0)


def local(snapshot):
    xlocal, ylocal, zlocal = snapshot.shape
    groups = lax.axis_size("gx")
    per = ylocal // groups
    chunks = chunk_count(per)
    steps = per // chunks
    starts = [chunk * steps for chunk in range(chunks)]
    me = lax.axis_index("gx").astype(jnp.int32).reshape(1)
    core = lax.axis_index(CORES).astype(jnp.int32).reshape(1)

    pieces = [(0, xlocal, start, steps) for start in starts]
    packed = pack(me, snapshot, groups, pieces[:1], LARGE)
    if chunks > 1:
        packed += [parts for piece in pieces[1:] for parts in pack(me, snapshot, groups, [piece], SMALL)]

    moved = []
    for index, parts in enumerate(packed):
        if index >= 2:
            parts = hold(parts, moved[index - 2])
        moved.append(exchange(parts))

    unit = math.lcm(2 * lax.axis_size(CHIPS), 2 * BLOCK)
    halves = []
    sums = [None]
    for index, parts in enumerate(moved):
        sums, made = gram_step(me, core, parts, sums[0], unit if index == chunks - 1 else None)
        halves.append(made)
    own, other = total_sum(*sums)
    mine, turned = factor_step(me, core, own, other, groups, xlocal)
    outs = []
    for held in halves[-1:] + halves[:-1]:
        if len(outs) == 1:
            (turned,) = hold([turned], parts[0])
        parts = core_step(me, turned, held, groups, zlocal)
        outs.append(exchange(hold(parts, outs[-3]) if len(outs) >= 3 else parts))
    return (mine, place(me, outs, starts[-1:] + starts[:-1], ylocal))


def solution(mesh):
    gx, gy, gz = mesh.devices.shape
    mesh = jax.sharding.Mesh(mesh.devices.reshape(gx, gy, gz // 2, 2), (*CHIPS, CORES))
    grid = P("gx", "gy", ("gu", CORES))
    return jax.shard_map(local, mesh=mesh, in_specs=(grid,), out_specs=(P("gx", None), grid), check_vma=False)
```
